256 devices in a mesh: batch: 2 (over z_lo), ctx: 16 (over x, y), head: 8 (over z_hi, core).
Axes of the slice: x: 4, y: 4, z: 8 (z_hi: 4, z_lo: 2; z = z_hi * 2 + z_lo), core: 2. Of those that a mesh axis runs over, the one named last changes fastest.
Arguments:
- hidden: bfloat16 [2, 6144, 3072], P('batch', 'ctx', 'head'), may hold values from -6 to 6
- modulation: float32 [2, 3, 3072], P('batch'), may hold values from -3 to 3
- qkv_weight: bfloat16 [3072, 3, 3072], P('ctx', None, 'head'), may hold values from -0.109375 to 0.109375
- q_gain: float32 [128], replicated
- k_gain: float32 [128], replicated
- out_weight: bfloat16 [3072, 3072], P('head'), may hold values from -0.109375 to 0.109375
- control: bfloat16 [2, 6144, 3072], P('batch', 'ctx'), may hold values from -6 to 6
- zero_weight: bfloat16 [3072, 3072], P(None, 'head'), may hold values from -0.109375 to 0.109375
- zero_bias: float32 [3072], P('head'), may hold values from -3 to 3
- pattern: int32 [16, 24], replicated, may hold values from -1 to 15, as said below
- control_order: int32 [2, 6144], P('batch'), may hold values from 0 to 6143, each once within a row
Outputs:
- mixed: bfloat16 [2, 6144, 3072], P('batch', 'ctx', 'head')
The draws below stay inside these ranges and needn't reach their ends.
Inputs may be any that keep to these rules, and one draw needn't show every extreme that they name: `pattern`: tile number t * 8 + h * 8 + w sits at grid place (t, h, w). A row lists only tiles whose t differs from its own by at most 1, lists its own tile and the tiles at its own (h, w) in the neighbouring time steps, names no tile twice, and holds -1 in its other slots.
All inputs are finite; a program needn't handle non-finite values.
Results may differ from the reference program's by a relative error of at most 0.0096.
The reference program's roundings to bfloat16 on the way (of `modulated`, `values`, `weights`, `attended`, `control_residual` and `relayed`) count: a program that leaves them out, or rounds other values in their place, can miss the bound.
Values may be sent and summed in bfloat16 or wider, within the bound.
No kernel may reach another device: no remote copies, remote signals or barrier semaphores. Data moves between devices by JAX's collectives and lax.ppermute only.
A program may use at most 256 MiB of HBM per device.

```python
import math
import jax
import jax.numpy as jnp
from jax import lax

D = 3072
HEADS = 24
HEAD_DIM = 128
TILE = 384
GRID_H = 1
GRID_T = 2
TILES = 16
GRID_W = 8
SEQ = 6144
SLOTS = 24
BATCH = 2


def draw_q_gain(key, part):
    key = jax.random.fold_in(key, 11)
    return jnp.exp(jax.random.uniform(key, (HEAD_DIM,), jnp.float32, 0.0, math.log(4.0)))


def draw_k_gain(key, part):
    key = jax.random.fold_in(key, 23)
    return jax.random.uniform(key, (HEAD_DIM,), jnp.float32, 0.6, 1.4)


def draw_pattern(key, part):
    key = jax.random.fold_in(key, 37)
    plane = GRID_H * GRID_W
    tiles = jnp.arange(TILES, dtype=jnp.int32)
    slots = jnp.arange(SLOTS, dtype=jnp.int32)
    time_of = tiles // plane
    place_of = tiles % plane
    step_t = slots // plane - 1
    other = slots % plane
    target_t = time_of[:, None] + step_t[None, :]
    candidate = target_t * plane + other[None, :]
    inside = (target_t >= 0) & (target_t < GRID_T)
    itself = other[None, :] == place_of[:, None]
    key_level, key_roll = jax.random.split(key)
    level = jax.random.randint(key_level, (TILES, 1), 1, 5)
    roll = jax.random.randint(key_roll, (TILES, SLOTS), 0, 4)
    keep = inside & (itself | (roll < level))
    return jnp.where(keep, candidate, -1).astype(jnp.int32)


def shard_levels(stream_key, shape, cuts, least, top_value):
    level, own = 1.0, jax.random.fold_in(stream_key, 6)
    for position, parts in cuts:
        heights = jnp.exp(jax.random.uniform(jax.random.fold_in(own, position), (parts,), jnp.float32, least / len(cuts), top_value / len(cuts)))
        level = level * jnp.repeat(heights, shape[position] // parts).reshape([-1 if axis == position else 1 for axis in range(len(shape))])
    return level


def normal_values(rng, extent, scale, reach, cuts=(), kind=jnp.bfloat16):
    level = shard_levels(rng, extent, cuts, -0.22, 0.18) if cuts else 1.0
    result = jax.random.normal(rng, extent, jnp.float32) * scale * level
    return jnp.minimum(jnp.maximum(result, -reach), reach).astype(kind)


def setup_inputs(seed: int = 0) -> dict:
    arg_keys = jax.random.split(jax.random.key(seed), 12)
    return {
        "hidden": normal_values(arg_keys[0], (BATCH, SEQ, D), 1.0, 6.0, ((0, 2), (1, 16), (2, 8))),
        "modulation": normal_values(arg_keys[1], (BATCH, 3, D), 0.5, 3.0, ((0, 2),), jnp.float32),
        "qkv_weight": normal_values(arg_keys[2], (D, 3, D), D ** -0.5, 0.109375, ((0, 16), (2, 8))),
        "q_gain": draw_q_gain(jax.random.fold_in(arg_keys[11], 71), 0),
        "k_gain": draw_k_gain(jax.random.fold_in(arg_keys[11], 71), 0),
        "out_weight": normal_values(arg_keys[5], (D, D), D ** -0.5, 0.109375, ((0, 8),)),
        "control": normal_values(arg_keys[6], (BATCH, SEQ, D), 1.0, 6.0, ((0, 2), (1, 16))),
        "zero_weight": normal_values(arg_keys[7], (D, D), D ** -0.5, 0.109375, ((1, 8),)),
        "zero_bias": normal_values(arg_keys[8], (D,), 0.5, 3.0, ((0, 8),), jnp.float32),
        "pattern": draw_pattern(jax.random.fold_in(arg_keys[11], 71), 0),
        "control_order": jax.vmap(lambda own: jax.random.permutation(own, SEQ))(jax.random.split(arg_keys[10], BATCH)).reshape((BATCH, SEQ)).astype(jnp.int32),
    }


def norm_heads(block, gain):
    shaped = block.reshape(block.shape[0], HEADS, HEAD_DIM)
    factor = lax.rsqrt(lax.optimization_barrier(jnp.mean(shaped * shaped, axis=-1, keepdims=True)) + 1e-06)
    return (shaped * factor * gain).astype(jnp.bfloat16)

def reference(hidden, modulation, qkv_weight, q_gain, k_gain, out_weight, control, zero_weight, zero_bias, pattern, control_order):
    scale = 1.0 / math.sqrt(HEAD_DIM)
    results = []
    for sample in range(BATCH):
        values32 = hidden[sample].astype(jnp.float32)
        mean = lax.optimization_barrier(jnp.mean(values32, axis=-1, keepdims=True))
        centred = values32 - mean
        spread = lax.optimization_barrier(jnp.mean(centred * centred, axis=-1, keepdims=True))
        modulated = (centred * lax.rsqrt(spread + 1e-06) * (1.0 + modulation[sample, 1]) + modulation[sample, 0]).astype(jnp.bfloat16)
        projections = jnp.dot(modulated, qkv_weight.reshape(D, 3 * D), preferred_element_type=jnp.float32)
        queries = norm_heads(projections[:, :D], q_gain)
        keys = norm_heads(projections[:, D:2 * D], k_gain)
        values = projections[:, 2 * D:].astype(jnp.bfloat16).reshape(SEQ, HEADS, HEAD_DIM)

        def tile_out(item):
            tile, row = item
            query_tile = lax.dynamic_slice_in_dim(queries, (tile * TILE).astype(jnp.int32), TILE, 0).astype(jnp.float32)
            index = (jnp.maximum(row, 0)[:, None] * TILE + jnp.arange(TILE, dtype=jnp.int32)[None, :]).reshape(-1)
            valid = jnp.repeat(row >= 0, TILE)
            key_tile = keys[index].astype(jnp.float32)
            value_tile = values[index].astype(jnp.float32)
            scores = jnp.einsum('qhd,khd->hqk', query_tile, key_tile) * scale
            scores = jnp.where(valid[None, None, :], scores, -jnp.inf)
            top = lax.optimization_barrier(jnp.max(scores, axis=-1, keepdims=True))
            weights = jnp.exp(scores - top)
            total = lax.optimization_barrier(jnp.sum(weights, axis=-1))
            rounded = lax.optimization_barrier(weights.astype(jnp.bfloat16)).astype(jnp.float32)
            summed = jnp.einsum('hqk,khd->qhd', rounded, value_tile)
            return (summed / jnp.transpose(total)[:, :, None]).astype(jnp.bfloat16).reshape(TILE, D)
        attended = lax.map(tile_out, (jnp.arange(TILES, dtype=jnp.int32), pattern)).reshape(SEQ, D)
        projected = jnp.dot(attended, out_weight, preferred_element_type=jnp.float32)
        control_residual = (jnp.dot(control[sample], zero_weight, preferred_element_type=jnp.float32) + zero_bias).astype(jnp.bfloat16)
        relayed = control_residual[control_order[sample]]
        mixed = values32 + modulation[sample, 2] * projected + relayed.astype(jnp.float32)
        results.append(mixed.astype(jnp.bfloat16))
    return jnp.stack(results)
```

```python
import functools
import math

import jax
import jax.numpy as jnp
from jax import lax
from jax.experimental import pallas as pl
from jax.experimental.pallas import tpu as pltpu
from jax.sharding import PartitionSpec as P

HEAD_DIM = 128
TILE = 384
SIDE = 4
AROUND = (0, -1, 1, 2)
VMEM = pl.BlockSpec(memory_space=pltpu.VMEM)
SMEM = pl.BlockSpec(memory_space=pltpu.SMEM)
HBM = pl.BlockSpec(memory_space=pl.ANY)
LOG2E = math.log2(math.e)


def params(mib):
    return pltpu.CompilerParams(vmem_limit_bytes=mib << 20)


def ctx_shift(value, dx, dy):
    pairs = [
        (a * SIDE + b, ((a + dx) % SIDE) * SIDE + (b + dy) % SIDE)
        for a in range(SIDE)
        for b in range(SIDE)
    ]
    return lax.ppermute(value, "ctx", pairs)


def z_shift(value, dz):
    pairs = [(z * 2 + c, ((z + dz) % SIDE) * 2 + c) for z in range(SIDE) for c in range(2)]
    return lax.ppermute(value, "head", pairs)


def core_swap(value):
    return lax.ppermute(
        value, "head", [(z * 2 + c, z * 2 + 1 - c) for z in range(SIDE) for c in range(2)]
    )


def cut(value, axis, start, stop):
    return lax.slice_in_dim(value, start, stop, axis=axis)


def ring(shift, value, axis):
    half = value.shape[axis] // 2
    back, front = shift(value, 1), shift(value, -1)
    first = shift(cut(back, axis, 0, half), 1)
    second = shift(cut(front, axis, half, 2 * half), -1)
    return back, front, first, second


def gather(value, axis, x_first):
    def along_x(v, d):
        return ctx_shift(v, d, 0)

    def along_y(v, d):
        return ctx_shift(v, 0, d)

    one, two = (along_x, along_y) if x_first else (along_y, along_x)
    stack = jnp.concatenate((value,) + ring(one, value, axis), axis=axis)
    back, front, first, second = ring(two, stack, axis)

    def at(firsts, other):
        return tuple((f, other) if x_first else (other, f) for f in firsts)

    return [
        (stack, at(AROUND, 0)),
        (back, at(AROUND, -1)),
        (front, at(AROUND, 1)),
        (first, at(AROUND[:2], 2)),
        (second, at(AROUND[2:], 2)),
    ]


def modulate_kernel(near_ref, far_ref, mods_ref, places_ref, out_ref):
    rows, width = out_ref.shape[0], near_ref.shape[1]
    count = near_ref.shape[0] // rows
    total = jnp.zeros((rows, 1), jnp.float32)
    for ref in (near_ref, far_ref):
        for k in range(count):
            total += jnp.sum(
                ref[k * rows : (k + 1) * rows, :].astype(jnp.float32), axis=1, keepdims=True
            )
    mean = total / (2 * count * width)
    total = jnp.zeros((rows, 1), jnp.float32)
    for ref in (near_ref, far_ref):
        for k in range(count):
            centred = ref[k * rows : (k + 1) * rows, :].astype(jnp.float32) - mean
            total += jnp.sum(centred * centred, axis=1, keepdims=True)
    factor = lax.rsqrt(total / (2 * count * width) + 1e-06)
    for s, ref in enumerate((near_ref, far_ref)):
        for k in range(count):
            place = places_ref[s * count + k]
            centred = ref[k * rows : (k + 1) * rows, :].astype(jnp.float32) - mean
            block = centred * factor * (1.0 + mods_ref[1, place]) + mods_ref[0, place]
            columns = pl.ds(pl.multiple_of(place * width, width), width)
            out_ref[:, columns] = block.astype(jnp.bfloat16)


def project_kernel(tables, modulated_ref, q_gain_ref, k_gain_ref, places_ref, *refs):
    count = len(tables)
    pieces, (q_ref, kv_ref, weight, sem) = refs[:count], refs[count:]
    block = tables[0][1]
    copies = []
    number = 0
    for ref, (blocks, rows, offset) in zip(pieces, tables, strict=True):
        for k in range(blocks):
            start = pl.multiple_of(places_ref[number] * (2 * block) + offset, 16)
            copies.append(
                pltpu.make_async_copy(
                    ref.at[:, pl.ds(k * block, block), :],
                    weight.at[:, pl.ds(start, block), :],
                    sem.at[number],
                )
            )
            number += 1
    for copy in copies:
        copy.start()
    for copy in copies:
        copy.wait()
    width = q_ref.shape[1]
    modulated = modulated_ref[...]

    def normed(j, gain_ref):
        out = jnp.dot(modulated, weight[j], preferred_element_type=jnp.float32)
        parts = []
        for h in range(width // HEAD_DIM):
            part = out[:, h * HEAD_DIM : (h + 1) * HEAD_DIM]
            factor = lax.rsqrt(jnp.mean(part * part, axis=1, keepdims=True) + 1e-06)
            parts.append((part * factor * gain_ref[...]).astype(jnp.bfloat16))
        return jnp.concatenate(parts, axis=1)

    kv_ref[:, :width] = normed(1, k_gain_ref)
    kv_ref[:, width:] = jnp.dot(
        modulated, weight[2], preferred_element_type=jnp.float32
    ).astype(jnp.bfloat16)
    q_ref[...] = normed(0, q_gain_ref)


def attend(q_ref, flags_ref, pieces, acc, best, total):
    heads = q_ref.shape[1] // HEAD_DIM
    width = heads * HEAD_DIM
    half = TILE // 2
    scale = LOG2E / math.sqrt(HEAD_DIM)
    number = 0
    state = [(acc[h], best[h], total[h]) for h in range(heads)] if acc is not None else None
    lane = lax.broadcasted_iota(jnp.int32, (1, TILE), 1)
    for ref in pieces:
        for g in range(ref.shape[0] // TILE):
            low, high = flags_ref[number], flags_ref[number + 1]
            number += 2
            bias = jnp.where(jnp.where(lane < half, low, high) > 0, 0.0, -1e30)
            rows = pl.ds(g * TILE, TILE)
            fresh = []
            for h in range(heads):
                q = q_ref[:, h * HEAD_DIM : (h + 1) * HEAD_DIM]
                k = ref[rows, h * HEAD_DIM : (h + 1) * HEAD_DIM]
                v = ref[rows, width + h * HEAD_DIM : width + (h + 1) * HEAD_DIM]
                scores = lax.dot_general(
                    q, k, (((1,), (1,)), ((), ())), preferred_element_type=jnp.float32
                )
                scores = scores * scale + bias
                top = jnp.max(scores, axis=1, keepdims=True)
                if state is not None:
                    top = jnp.maximum(top, state[h][1])
                weights = jnp.exp2(scores - top)
                summed = jnp.sum(weights, axis=1, keepdims=True)
                update = jnp.dot(
                    weights.astype(jnp.bfloat16), v, preferred_element_type=jnp.float32
                )
                if state is not None:
                    factor = jnp.exp2(state[h][1] - top)
                    summed += state[h][2] * factor
                    update += state[h][0] * factor
                fresh.append((update, top, summed))
            state = fresh
    return state


def attend_kernel(count, first, q_ref, flags_ref, *refs):
    pieces, refs = refs[:count], refs[count:]
    if first:
        (acc_ref, best_ref, total_ref) = refs
        state = attend(q_ref, flags_ref, pieces, None, None, None)
    else:
        (acc_in, best_in, total_in, acc_ref, best_ref, total_ref) = refs
        state = attend(q_ref, flags_ref, pieces, acc_in, best_in, total_in)
    for h, (acc, best, total) in enumerate(state):
        acc_ref[h], best_ref[h], total_ref[h] = acc, best, total


def finish_kernel(
    count, q_ref, flags_ref, places_ref, out_weight_ref, acc_in, best_in, total_in, *refs
):
    pieces, (near_ref, far_ref) = refs[:count], refs[count:]
    state = attend(q_ref, flags_ref, pieces, acc_in, best_in, total_in)
    attended = jnp.concatenate(
        [(acc / total).astype(jnp.bfloat16) for acc, _, total in state], axis=1
    )
    width = near_ref.shape[2]
    slots = near_ref.shape[0]
    for s, ref in enumerate((far_ref, near_ref)):
        for k in range(slots):
            place = places_ref[(1 - s) * slots + k]
            columns = pl.ds(pl.multiple_of(place * width, width), width)
            ref[k] = jnp.dot(
                attended, out_weight_ref[:, columns], preferred_element_type=jnp.float32
            ).astype(ref.dtype)


def control_kernel(control_ref, weight_ref, bias_ref, out_ref):
    out = jnp.dot(control_ref[...], weight_ref[...], preferred_element_type=jnp.float32)
    out_ref[...] = (out + bias_ref[...]).astype(jnp.bfloat16)


def pick_kernel(tables, wanted_ref, places_ref, *refs):
    count = len(tables)
    pieces, out_ref = refs[:count], refs[count]
    wanted = wanted_ref[...]
    number = 0
    total = jnp.zeros(out_ref.shape, jnp.float32)
    for ref, (blocks, rows, offset) in zip(pieces, tables, strict=True):
        lane = lax.broadcasted_iota(jnp.int32, (1, blocks * rows), 1)
        here = lane
        for k in range(blocks):
            start = places_ref[number] * (2 * rows) + offset - k * rows
            here = jnp.where((lane >= k * rows) & (lane < (k + 1) * rows), lane + start, here)
            number += 1
        hit = jnp.where(wanted == here, 1.0, 0.0).astype(jnp.bfloat16)
        total += jnp.dot(hit, ref[...], preferred_element_type=jnp.float32)
    out_ref[...] = total


def shaped(shape, dtype):
    return jax.ShapeDtypeStruct(shape, dtype)


def body(
    hidden,
    modulation,
    qkv_weight,
    q_gain,
    k_gain,
    out_weight,
    control,
    zero_weight,
    zero_bias,
    pattern,
    control_order,
):
    rows, cols = hidden.shape[1:]
    heads = cols // HEAD_DIM
    ctx_place, head_place = lax.axis_index("ctx"), lax.axis_index("head")
    x, y = ctx_place // SIDE, ctx_place % SIDE
    z, core = head_place // 2, head_place % 2
    own_rows = hidden[0]
    features = modulation.shape[2]
    mods = modulation[0].reshape(3, features // cols, 1, cols)

    def ctx_of(ox, oy):
        return ((x + ox) % SIDE) * SIDE + (y + oy) % SIDE

    def ctx_places(places):
        return jnp.stack([ctx_of(*p) for p in places]).astype(jnp.int32)

    head_places = jnp.stack(
        [((z + o) % SIDE) * 2 + c for c in (core, 1 - core) for o in AROUND]
    ).astype(jnp.int32)

    near = jnp.concatenate((own_rows,) + ring(z_shift, own_rows, 0), axis=0)
    far = core_swap(near)

    weight = jnp.transpose(qkv_weight, (1, 0, 2))
    half = weight.shape[1] // 2
    gathered = [gather(cut(weight, 1, 0, half), 1, True), gather(cut(weight, 1, half, 2 * half), 1, False)]
    pieces = [(piece, places, s * half) for s in range(2) for piece, places in gathered[s]]

    modulated = pl.pallas_call(
        modulate_kernel,
        out_shape=shaped((rows, features), jnp.bfloat16),
        in_specs=[VMEM, VMEM, VMEM, SMEM],
        out_specs=VMEM,
        compiler_params=params(32),
        name="modulate",
    )(near, far, mods, head_places)

    tables = [(len(places), half, offset) for _, places, offset in pieces]
    q, kv = pl.pallas_call(
        functools.partial(project_kernel, tables),
        out_shape=[shaped((rows, cols), jnp.bfloat16), shaped((rows, 2 * cols), jnp.bfloat16)],
        in_specs=[VMEM, VMEM, VMEM, SMEM] + [HBM] * len(pieces),
        out_specs=[VMEM, VMEM],
        scratch_shapes=[
            pltpu.VMEM((3, features, cols), jnp.bfloat16),
            pltpu.SemaphoreType.DMA((sum(t[0] for t in tables),)),
        ],
        compiler_params=params(32),
        name="project",
    )(
        modulated,
        q_gain.reshape(1, HEAD_DIM),
        k_gain.reshape(1, HEAD_DIM),
        jnp.concatenate([ctx_places(places) for _, places, _ in pieces]),
        *[piece for piece, _, _ in pieces],
    )

    listed = lax.dynamic_slice_in_dim(pattern, ctx_place, 1, 0)[0]
    allowed = jnp.any(
        listed[:, None] == jnp.arange(pattern.shape[0], dtype=jnp.int32)[None, :], axis=0
    ).astype(jnp.int32)
    half = rows // 2
    parts = [gather(kv[:half], 0, True), gather(kv[half:], 0, False)]

    def step(numbers):
        chosen = [part[i] for i in numbers for part in parts]
        return [c[0] for c in chosen], jnp.concatenate(
            [allowed[ctx_places(c[1])] for c in chosen]
        )

    state_shape = [
        shaped((heads, rows, HEAD_DIM), jnp.float32),
        shaped((heads, rows, 1), jnp.float32),
        shaped((heads, rows, 1), jnp.float32),
    ]
    state = []
    for numbers in ((0,), (1, 2)):
        chosen, flags = step(numbers)
        state = pl.pallas_call(
            functools.partial(attend_kernel, len(chosen), not state),
            out_shape=state_shape,
            in_specs=[VMEM, SMEM] + [VMEM] * (len(chosen) + len(state)),
            out_specs=[VMEM] * 3,
            compiler_params=params(40),
            name="attend",
        )(q, flags, *chosen, *state)
    chosen, flags = step((3, 4))
    near_terms, far_terms = pl.pallas_call(
        functools.partial(finish_kernel, len(chosen)),
        out_shape=[
            shaped((SIDE, rows, cols), jnp.float32),
            shaped((SIDE, rows, cols), jnp.bfloat16),
        ],
        in_specs=[VMEM, SMEM, SMEM, VMEM] + [VMEM] * (3 + len(chosen)),
        out_specs=[VMEM] * 2,
        compiler_params=params(40),
        name="finish",
    )(q, flags, head_places, out_weight, *state, *chosen)

    terms = near_terms + core_swap(far_terms).astype(jnp.float32)
    own_term, back_term, front_term, across_term = (terms[k] for k in range(SIDE))
    narrow = jnp.bfloat16
    half = rows // 2
    from_back = z_shift(across_term[:half].astype(narrow), 1)
    from_front = z_shift(across_term[half:].astype(narrow), -1)
    sums = [
        z_shift(front_term[half:].astype(narrow), 1),
        z_shift(back_term[:half].astype(narrow), -1),
        z_shift((front_term[:half] + from_back.astype(jnp.float32)).astype(narrow), 1),
        z_shift((back_term[half:] + from_front.astype(jnp.float32)).astype(narrow), -1),
    ]
    sums = [s.astype(jnp.float32) for s in sums]
    projected = (
        own_term
        + jnp.concatenate([sums[2], sums[0]], axis=0)
        + jnp.concatenate([sums[1], sums[3]], axis=0)
    )

    residual = pl.pallas_call(
        control_kernel,
        out_shape=shaped((rows, cols), jnp.bfloat16),
        in_specs=[VMEM] * 3,
        out_specs=VMEM,
        compiler_params=params(32),
        name="control",
    )(control[0], zero_weight, zero_bias.reshape(1, cols))
    half = rows // 2
    gathered = [gather(residual[:half], 0, True), gather(residual[half:], 0, False)]
    pieces = [(piece, places, s * half) for s in range(2) for piece, places in gathered[s]]
    tables = [(len(places), half, offset) for _, places, offset in pieces]
    wanted = lax.dynamic_slice_in_dim(control_order[0], ctx_place * rows, rows, 0)
    relayed = pl.pallas_call(
        functools.partial(pick_kernel, tables),
        out_shape=shaped((rows, cols), jnp.float32),
        in_specs=[VMEM, SMEM] + [VMEM] * len(pieces),
        out_specs=VMEM,
        compiler_params=params(32),
        name="pick",
    )(
        wanted.reshape(rows, 1),
        jnp.concatenate([ctx_places(places) for _, places, _ in pieces]),
        *[piece for piece, _, _ in pieces],
    )

    gate = lax.dynamic_slice_in_dim(modulation[0, 2], head_place * cols, cols, 0)
    mixed = own_rows.astype(jnp.float32) + gate * projected + relayed
    return mixed.astype(jnp.bfloat16)[None]


def solution(mesh):
    in_specs = (
        P("batch", "ctx", "head"),
        P("batch", None, None),
        P("ctx", None, "head"),
        P(),
        P(),
        P("head", None),
        P("batch", "ctx", None),
        P(None, "head"),
        P("head"),
        P(),
        P("batch", None),
    )
    out_specs = P("batch", "ctx", "head")
    return jax.shard_map(body, mesh=mesh, in_specs=in_specs, out_specs=out_specs, check_vma=False)
```

```python
import functools
import math

import jax
import jax.numpy as jnp
import numpy as np
from jax import lax
from jax.experimental import pallas as pl
from jax.experimental.pallas import tpu as pltpu
from jax.sharding import PartitionSpec as P

HEAD_DIM = 128
TILE = 384
SIDE = 4
AROUND = (0, -1, 1, 2)
VMEM = pl.BlockSpec(memory_space=pltpu.VMEM)
SMEM = pl.BlockSpec(memory_space=pltpu.SMEM)
HBM = pl.BlockSpec(memory_space=pl.ANY)
LOG2E = math.log2(math.e)


def cost(time):
    return pl.CostEstimate(flops=int(time * 1.15e9), bytes_accessed=0, transcendentals=0)


def params(mib):
    return pltpu.CompilerParams(vmem_limit_bytes=mib << 20)


def ctx_shift(value, axis, step):
    pairs = []
    for a in range(SIDE):
        for b in range(SIDE):
            for head in range(2 * SIDE):
                to = [a, b]
                along = (axis + head) % 2
                to[along] = (to[along] + step) % SIDE
                pairs.append(
                    ((a * SIDE + b) * 2 * SIDE + head, (to[0] * SIDE + to[1]) * 2 * SIDE + head)
                )
    return lax.ppermute(value, ("ctx", "head"), pairs)


def z_shift(value, dz):
    pairs = [(z * 2 + c, ((z + dz) % SIDE) * 2 + c) for z in range(SIDE) for c in range(2)]
    return lax.ppermute(value, "head", pairs)


def core_swap(value):
    return lax.ppermute(
        value, "head", [(z * 2 + c, z * 2 + 1 - c) for z in range(SIDE) for c in range(2)]
    )


def cut(value, axis, start, stop):
    return lax.slice_in_dim(value, start, stop, axis=axis)


def first_way(value, step):
    return ctx_shift(value, 0, step)


def second_way(value, step):
    return ctx_shift(value, 1, step)


def near(shift, value):
    return shift(value, 1), shift(value, -1)


def across(shift, back, front, axis):
    half = back.shape[axis] // 2
    return (
        shift(cut(back, axis, 0, half), 1),
        shift(cut(front, axis, half, 2 * half), -1),
    )


def after(value, *others):
    return lax.optimization_barrier((value,) + others)[0]


class Gather:
    def __init__(self, value, axis):
        self.value, self.axis = value, axis

    def start(self):
        self.sides = near(first_way, self.value)

    def gather_one(self):
        back, front = self.sides
        self.stack = jnp.concatenate(
            (self.value, back, front, first_way(back, 1)), axis=self.axis
        )

    def gather_near(self, *others):
        self.back, self.front = near(second_way, after(self.stack, *others))

    def gather_across(self, *others):
        self.first, self.second = across(
            second_way, after(self.back, *others), after(self.front, *others), self.axis
        )

    def pieces(self, start=0, stop=5):
        return [getattr(self, name) for name, _, _ in PIECES[start:stop]]


PIECES = (
    ("stack", AROUND, 0),
    ("back", AROUND, -1),
    ("front", AROUND, 1),
    ("first", AROUND[:2], 2),
    ("second", AROUND[2:], 2),
)


def distances(start=0, stop=5):
    return [(one, two) for _, ones, two in PIECES[start:stop] for one in ones]


def modulate_kernel(near_ref, far_ref, mods_ref, slots_ref, out_ref):
    rows, width = out_ref.shape[0], near_ref.shape[1]
    count = near_ref.shape[0] // rows
    blocks = slots_ref.shape[1]
    half = out_ref.shape[1] // blocks
    total = jnp.zeros((rows, HEAD_DIM), jnp.float32)
    for ref in (near_ref, far_ref):
        for k in range(count):
            for n in range(width // HEAD_DIM):
                total += ref[
                    k * rows : (k + 1) * rows, n * HEAD_DIM : (n + 1) * HEAD_DIM
                ].astype(jnp.float32)
    mean = jnp.sum(total, axis=1, keepdims=True) / (2 * count * width)
    total = jnp.zeros((rows, HEAD_DIM), jnp.float32)
    for ref in (near_ref, far_ref):
        for k in range(count):
            for n in range(width // HEAD_DIM):
                centred = (
                    ref[k * rows : (k + 1) * rows, n * HEAD_DIM : (n + 1) * HEAD_DIM].astype(
                        jnp.float32
                    )
                    - mean
                )
                total += centred * centred
    spread = jnp.sum(total, axis=1, keepdims=True) / (2 * count * width)
    factor = lax.rsqrt(spread + 1e-06)
    for n in range(blocks):
        slot, late, place = slots_ref[0, n], slots_ref[1, n], slots_ref[2, n]
        at = pl.ds(pl.multiple_of((slot % count) * rows, rows), rows)
        block = jnp.where(slot < count, near_ref[at, :], far_ref[at, :])
        block = jnp.where(late > 0, block[:, half:], block[:, :half]).astype(jnp.float32)
        block = (block - mean) * factor * (1.0 + mods_ref[1, place]) + mods_ref[0, place]
        out_ref[:, n * half : (n + 1) * half] = block.astype(jnp.bfloat16)


def project(modulated_ref, pieces, j):
    out, start = None, 0
    for ref in pieces:
        depth = ref.shape[1]
        term = jnp.dot(
            modulated_ref[:, start : start + depth], ref[j], preferred_element_type=jnp.float32
        )
        out = term if out is None else out + term
        start += depth
    return out


def norm_heads(out, gain_ref):
    parts = []
    for h in range(out.shape[1] // HEAD_DIM):
        part = out[:, h * HEAD_DIM : (h + 1) * HEAD_DIM]
        factor = lax.rsqrt(jnp.mean(part * part, axis=1, keepdims=True) + 1e-06)
        parts.append((part * factor * gain_ref[...]).astype(jnp.bfloat16))
    return jnp.concatenate(parts, axis=1)


def keys_kernel(modulated_ref, gain_ref, *refs):
    pieces, (k_ref, v_ref) = refs[:-2], refs[-2:]
    k_ref[...] = norm_heads(project(modulated_ref, pieces, 0), gain_ref)
    v_ref[...] = project(modulated_ref, pieces, 1).astype(jnp.bfloat16)


def queries_kernel(modulated_ref, gain_ref, *refs):
    pieces, q_ref = refs[:-1], refs[-1]
    q_ref[...] = norm_heads(project(modulated_ref, pieces, 0), gain_ref)


def attend(q_ref, allowed_ref, places_ref, pieces, acc, best, total):
    heads = q_ref.shape[1] // HEAD_DIM
    scale = LOG2E / math.sqrt(HEAD_DIM)
    half = len(pieces) // 2
    groups = [
        (k_ref, v_ref, pl.ds(g * TILE, TILE))
        for k_ref, v_ref in zip(pieces[:half], pieces[half:], strict=True)
        for g in range(k_ref.shape[0] // TILE)
    ]
    biases = [
        jnp.where(allowed_ref[places_ref[n]] > 0, 0.0, -1e30).astype(jnp.float32)
        for n in range(len(groups))
    ]
    state = []
    for h in range(heads):
        mine = slice(h * HEAD_DIM, (h + 1) * HEAD_DIM)
        q = q_ref[:, mine]
        scores = []
        widest = None
        for (ref, _, rows), bias in zip(groups, biases, strict=True):
            part = (
                lax.dot_general(
                    q, ref[rows, mine], (((1,), (1,)), ((), ())), preferred_element_type=jnp.float32
                )
                + bias
            )
            scores.append(part)
            for n in range(TILE // HEAD_DIM):
                lanes = part[:, n * HEAD_DIM : (n + 1) * HEAD_DIM]
                widest = lanes if widest is None else jnp.maximum(widest, lanes)
        top = jnp.max(widest, axis=1, keepdims=True)
        if acc is not None:
            top = jnp.maximum(top, best[h])
        summed, update = None, None
        for (_, ref, rows), part in zip(groups, scores, strict=True):
            weights = jnp.exp2((part - top) * scale)
            for n in range(TILE // HEAD_DIM):
                lanes = weights[:, n * HEAD_DIM : (n + 1) * HEAD_DIM]
                summed = lanes if summed is None else summed + lanes
            term = jnp.dot(
                weights.astype(jnp.bfloat16), ref[rows, mine], preferred_element_type=jnp.float32
            )
            update = term if update is None else update + term
        summed = jnp.sum(summed, axis=1, keepdims=True)
        if acc is not None:
            factor = jnp.exp2((best[h] - top) * scale)
            summed += total[h] * factor
            update += acc[h] * factor
        state.append((update, top, summed))
    return state


def attend_kernel(count, first, q_ref, allowed_ref, places_ref, *refs):
    pieces, refs = refs[:count], refs[count:]
    if first:
        (acc_ref, best_ref, total_ref) = refs
        state = attend(q_ref, allowed_ref, places_ref, pieces, None, None, None)
    else:
        (acc_in, best_in, total_in, acc_ref, best_ref, total_ref) = refs
        state = attend(q_ref, allowed_ref, places_ref, pieces, acc_in, best_in, total_in)
    for h, (acc, best, total) in enumerate(state):
        acc_ref[h], best_ref[h], total_ref[h] = acc, best, total


def project_out(attended, out_weight_ref, places_ref, first, ref):
    slots, _, width = ref.shape
    for k in range(slots):
        columns = pl.ds(pl.multiple_of(places_ref[first + k] * width, width), width)
        ref[k] = jnp.dot(
            attended, out_weight_ref[:, columns], preferred_element_type=jnp.float32
        ).astype(ref.dtype)


def finish_kernel(
    count,
    q_ref,
    allowed_ref,
    tiles_ref,
    places_ref,
    out_weight_ref,
    acc_in,
    best_in,
    total_in,
    *refs,
):
    pieces, (attended_ref, far_ref) = refs[:count], refs[count:]
    state = attend(q_ref, allowed_ref, tiles_ref, pieces, acc_in, best_in, total_in)
    attended = jnp.concatenate(
        [(acc / total).astype(jnp.bfloat16) for acc, _, total in state], axis=1
    )
    attended_ref[...] = attended
    project_out(attended, out_weight_ref, places_ref, far_ref.shape[0], far_ref)


def near_kernel(attended_ref, places_ref, out_weight_ref, near_ref):
    project_out(attended_ref[...], out_weight_ref, places_ref, 0, near_ref)


def cores_kernel(near_ref, far_ref, own_ref, later_ref, up_ref, down_ref):
    half = near_ref.shape[1] // 2
    first, second = slice(0, half), slice(half, 2 * half)

    def both(k, rows):
        return near_ref[k, rows, :] + far_ref[k, rows, :].astype(jnp.float32)

    for rows in (first, second):
        own_ref[rows, :] = both(0, rows)
    later_ref[first, :] = both(2, first)
    later_ref[second, :] = both(1, second)
    up_ref[first, :] = both(3, first).astype(jnp.bfloat16)
    up_ref[second, :] = both(2, second).astype(jnp.bfloat16)
    down_ref[first, :] = both(1, first).astype(jnp.bfloat16)
    down_ref[second, :] = both(3, second).astype(jnp.bfloat16)


def control_kernel(control_ref, weight_ref, bias_ref, out_ref):
    out = jnp.dot(control_ref[...], weight_ref[...], preferred_element_type=jnp.float32)
    out_ref[...] = (out + bias_ref[...]).astype(jnp.bfloat16)


def pick_kernel(wanted_ref, places_ref, *refs):
    half = len(refs) // 2
    rows = refs[0].shape[0]
    lane = lax.broadcasted_iota(jnp.int32, (1, rows), 1)
    for n, out_ref in enumerate(refs[half:]):
        wanted = wanted_ref[n * rows : (n + 1) * rows, :]
        total = jnp.zeros(out_ref.shape, jnp.float32)
        for k, ref in enumerate(refs[:half]):
            hit = jnp.where(wanted == lane + places_ref[k] * rows, 1.0, 0.0).astype(jnp.bfloat16)
            total += jnp.dot(hit, ref[...], preferred_element_type=jnp.float32)
        out_ref[...] = total.astype(out_ref.dtype)


def shaped(shape, dtype):
    return jax.ShapeDtypeStruct(shape, dtype)


def body(
    hidden,
    modulation,
    qkv_weight,
    q_gain,
    k_gain,
    out_weight,
    control,
    zero_weight,
    zero_bias,
    pattern,
    control_order,
):
    rows, cols = hidden.shape[1:]
    heads = cols // HEAD_DIM
    ctx_place, head_place = lax.axis_index("ctx"), lax.axis_index("head")
    x, y = ctx_place // SIDE, ctx_place % SIDE
    z, core = head_place // 2, head_place % 2
    own_rows = hidden[0]
    features = modulation.shape[2]
    mods = modulation[0].reshape(3, 2 * features // cols, 1, cols // 2)

    def ctx_of(one, two):
        return jnp.where(
            core == 0,
            ((x + one) % SIDE) * SIDE + (y + two) % SIDE,
            ((x + two) % SIDE) * SIDE + (y + one) % SIDE,
        )

    def ctx_places(places):
        ox, oy = (np.array(o, np.int32) for o in zip(*places))
        return ctx_of(ox, oy).astype(jnp.int32)

    head_places = jnp.stack(
        [((z + o) % SIDE) * 2 + c for c in (core, 1 - core) for o in AROUND]
    ).astype(jnp.int32)

    sides = near(z_shift, own_rows)
    weight = jnp.transpose(qkv_weight, (1, 0, 2))
    kv_weight, q_weight = Gather(weight[1:], 1), Gather(weight[:1], 1)
    kv_weight.start()
    kv_weight.gather_one()
    q_weight.start()
    kv_weight.gather_near(*sides)
    ends = across(z_shift, *sides, 0)
    near_rows = jnp.concatenate((own_rows,) + sides + ends, axis=0)
    far_rows = core_swap(near_rows)
    q_weight.gather_one()
    kv_weight.gather_across(near_rows, q_weight.stack)
    q_weight.gather_near()

    residual = pl.pallas_call(
        control_kernel,
        out_shape=shaped((rows, cols), jnp.bfloat16),
        in_specs=[VMEM] * 3,
        out_specs=VMEM,
        compiler_params=params(32),
        cost_estimate=cost(3),
        name="control",
    )(control[0], zero_weight, after(zero_bias, kv_weight.stack).reshape(1, cols))
    residuals = (residual,) + near(first_way, residual) + (first_way(residual, 2),)

    order = ctx_places(distances())
    place = order // 2
    slot = jnp.array([0, 2, 3, 1], jnp.int32)[(place // 2 - z) % SIDE]
    slot += jnp.where(place % 2 == core, 0, SIDE).astype(jnp.int32)
    modulated = pl.pallas_call(
        modulate_kernel,
        out_shape=shaped((rows, features), jnp.bfloat16),
        in_specs=[VMEM, VMEM, VMEM, SMEM],
        out_specs=VMEM,
        compiler_params=params(32),
        cost_estimate=cost(5),
        name="modulate",
    )(near_rows, far_rows, mods, jnp.stack([slot, order % 2, order]))

    k, v = pl.pallas_call(
        keys_kernel,
        out_shape=[shaped((rows, cols), jnp.bfloat16)] * 2,
        in_specs=[VMEM] * 7,
        out_specs=[VMEM] * 2,
        compiler_params=params(32),
        cost_estimate=cost(6),
        name="keys",
    )(modulated, k_gain.reshape(1, HEAD_DIM), *kv_weight.pieces())
    k, v, *residuals = lax.optimization_barrier((k, v, *residuals))

    listed = lax.dynamic_slice_in_dim(pattern, ctx_place, 1, 0)[0]
    allowed = jnp.any(
        listed[:, None] == jnp.arange(pattern.shape[0], dtype=jnp.int32)[None, :], axis=0
    ).astype(jnp.int32)
    keys, values = Gather(k, 0), Gather(v, 0)
    keys.start()
    values.start()
    keys.gather_one()
    values.gather_one()
    q_weight.gather_across(k)
    keys.gather_near()
    values.gather_near()
    q = pl.pallas_call(
        queries_kernel,
        out_shape=shaped((rows, cols), jnp.bfloat16),
        in_specs=[VMEM] * 7,
        out_specs=VMEM,
        compiler_params=params(32),
        cost_estimate=cost(4),
        name="queries",
    )(modulated, q_gain.reshape(1, HEAD_DIM), *q_weight.pieces())

    state_shape = [
        shaped((heads, rows, HEAD_DIM), jnp.float32),
        shaped((heads, rows, 1), jnp.float32),
        shaped((heads, rows, 1), jnp.float32),
    ]
    def attention(start, stop, state, time):
        chosen = keys.pieces(start, stop) + values.pieces(start, stop)
        return pl.pallas_call(
            functools.partial(attend_kernel, len(chosen), not state),
            out_shape=state_shape,
            in_specs=[VMEM, SMEM, SMEM] + [VMEM] * (len(chosen) + len(state)),
            out_specs=[VMEM] * 3,
            compiler_params=params(48),
            cost_estimate=cost(time),
            name="attend",
        )(q, allowed, ctx_places(distances(start, stop)), *chosen, *state)

    state = attention(0, 1, [], 5)

    wanted = jnp.concatenate(
        [
            lax.dynamic_slice_in_dim(control_order[0], ctx_of(0, o) * rows, rows, 0)
            for o in (0, 1, -1, 2)
        ]
    )
    relayed = pl.pallas_call(
        pick_kernel,
        out_shape=[shaped((rows, cols), jnp.bfloat16)] * SIDE,
        in_specs=[VMEM, SMEM] + [VMEM] * SIDE,
        out_specs=[VMEM] * SIDE,
        compiler_params=params(32),
        cost_estimate=cost(5),
        name="pick",
    )(
        wanted.reshape(SIDE * rows, 1),
        ctx_places([(o, 0) for o in AROUND]),
        *residuals,
    )
    keys.gather_across(state[2], relayed[0])
    values.gather_across()
    state = attention(1, 3, state, 10)
    chosen = keys.pieces(3, 5) + values.pieces(3, 5)
    attended, far_terms = pl.pallas_call(
        functools.partial(finish_kernel, len(chosen)),
        out_shape=[
            shaped((rows, cols), jnp.bfloat16),
            shaped((SIDE, rows, cols), jnp.bfloat16),
        ],
        in_specs=[VMEM, SMEM, SMEM, SMEM, VMEM] + [VMEM] * (3 + len(chosen)),
        out_specs=[VMEM] * 2,
        compiler_params=params(48),
        cost_estimate=cost(8),
        name="finish",
    )(q, allowed, ctx_places(distances(3, 5)), head_places, out_weight, *state, *chosen)
    near_terms = pl.pallas_call(
        near_kernel,
        out_shape=shaped((SIDE, rows, cols), jnp.float32),
        in_specs=[VMEM, SMEM, VMEM],
        out_specs=VMEM,
        compiler_params=params(32),
        cost_estimate=cost(2),
        name="near",
    )(attended, head_places, out_weight)

    own_term, later, up, down = pl.pallas_call(
        cores_kernel,
        out_shape=[shaped((rows, cols), jnp.float32)] * 2 + [shaped((rows, cols), jnp.bfloat16)] * 2,
        in_specs=[VMEM] * 2,
        out_specs=[VMEM] * 4,
        compiler_params=params(32),
        cost_estimate=cost(2),
        name="cores",
    )(near_terms, core_swap(far_terms))
    half = rows // 2
    up, down = z_shift(up, 1).astype(jnp.float32), z_shift(down, -1).astype(jnp.float32)
    late_up = z_shift((later[:half] + up[:half]).astype(jnp.bfloat16), 1)
    late_down = z_shift((later[half:] + down[half:]).astype(jnp.bfloat16), -1)
    projected = (
        own_term
        + jnp.concatenate([late_up.astype(jnp.float32), up[half:]], axis=0)
        + jnp.concatenate([down[:half], late_down.astype(jnp.float32)], axis=0)
    )

    kept, *sent = relayed
    sent = second_way(sent[0], 1), second_way(sent[1], -1), second_way(sent[2], 2)
    relayed = sum((r.astype(jnp.float32) for r in sent), kept.astype(jnp.float32))

    gate = lax.dynamic_slice_in_dim(modulation[0, 2], head_place * cols, cols, 0)
    mixed = own_rows.astype(jnp.float32) + gate * projected + relayed
    return mixed.astype(jnp.bfloat16)[None]


def solution(mesh):
    in_specs = (
        P("batch", "ctx", "head"),
        P("batch", None, None),
        P("ctx", None, "head"),
        P(),
        P(),
        P("head", None),
        P("batch", "ctx", None),
        P(None, "head"),
        P("head"),
        P(),
        P("batch", None),
    )
    out_specs = P("batch", "ctx", "head")
    return jax.shard_map(body, mesh=mesh, in_specs=in_specs, out_specs=out_specs, check_vma=False)
```

```python
import functools
import math

import jax
import jax.numpy as jnp
import numpy as np
from jax import lax
from jax.experimental import pallas as pl
from jax.experimental.pallas import tpu as pltpu
from jax.sharding import PartitionSpec as P

HEAD_DIM = 128
TILE = 384
SIDE = 4
AROUND = (0, -1, 1, 2)
VMEM = pl.BlockSpec(memory_space=pltpu.VMEM)
SMEM = pl.BlockSpec(memory_space=pltpu.SMEM)
HBM = pl.BlockSpec(memory_space=pl.ANY)
LOG2E = math.log2(math.e)


def cost(time):
    return pl.CostEstimate(flops=int(time * 1.15e9), bytes_accessed=0, transcendentals=0)


def params(mib):
    return pltpu.CompilerParams(vmem_limit_bytes=mib << 20)


def ctx_shift(value, axis, step):
    pairs = []
    for a in range(SIDE):
        for b in range(SIDE):
            for head in range(2 * SIDE):
                to = [a, b]
                along = (axis + head) % 2
                to[along] = (to[along] + step) % SIDE
                pairs.append(
                    ((a * SIDE + b) * 2 * SIDE + head, (to[0] * SIDE + to[1]) * 2 * SIDE + head)
                )
    return lax.ppermute(value, ("ctx", "head"), pairs)


def z_shift(value, dz):
    pairs = [(z * 2 + c, ((z + dz) % SIDE) * 2 + c) for z in range(SIDE) for c in range(2)]
    return lax.ppermute(value, "head", pairs)


def core_swap(value):
    return lax.ppermute(
        value, "head", [(z * 2 + c, z * 2 + 1 - c) for z in range(SIDE) for c in range(2)]
    )


def cut(value, axis, start, stop):
    return lax.slice_in_dim(value, start, stop, axis=axis)


def first_way(value, step):
    return ctx_shift(value, 0, step)


def second_way(value, step):
    return ctx_shift(value, 1, step)


def near(shift, value):
    return shift(value, 1), shift(value, -1)


def across(shift, back, front, axis):
    half = back.shape[axis] // 2
    return (
        shift(cut(back, axis, 0, half), 1),
        shift(cut(front, axis, half, 2 * half), -1),
    )


def after(value, *others):
    return lax.optimization_barrier((value,) + others)[0]


def first_step(value):
    back, front = near(first_way, value)
    return value, back, front, first_way(back, 1)


class Gather:
    def __init__(self, values, axis):
        self.axis = axis
        self.stack = jnp.concatenate(values, axis=axis)

    def gather_near(self, *others):
        self.back, self.front = near(second_way, after(self.stack, *others))

    def gather_across(self, *others):
        self.first, self.second = across(
            second_way, after(self.back, *others), after(self.front, *others), self.axis
        )

    def pieces(self, start=0, stop=5):
        return [getattr(self, name) for name in PIECES[start:stop]]


PIECES = ("stack", "back", "front", "first", "second")


def modulate_kernel(near_ref, far_ref, mods_ref, slots_ref, out_ref):
    rows, width = out_ref.shape[0], near_ref.shape[1]
    count = near_ref.shape[0] // rows
    blocks = slots_ref.shape[1]
    half = out_ref.shape[1] // blocks
    total = jnp.zeros((rows, HEAD_DIM), jnp.float32)
    for ref in (near_ref, far_ref):
        for k in range(count):
            for n in range(width // HEAD_DIM):
                total += ref[
                    k * rows : (k + 1) * rows, n * HEAD_DIM : (n + 1) * HEAD_DIM
                ].astype(jnp.float32)
    mean = jnp.sum(total, axis=1, keepdims=True) / (2 * count * width)
    total = jnp.zeros((rows, HEAD_DIM), jnp.float32)
    for ref in (near_ref, far_ref):
        for k in range(count):
            for n in range(width // HEAD_DIM):
                centred = (
                    ref[k * rows : (k + 1) * rows, n * HEAD_DIM : (n + 1) * HEAD_DIM].astype(
                        jnp.float32
                    )
                    - mean
                )
                total += centred * centred
    spread = jnp.sum(total, axis=1, keepdims=True) / (2 * count * width)
    factor = lax.rsqrt(spread + 1e-06)
    for n in range(blocks):
        slot, late, place = slots_ref[0, n], slots_ref[1, n], slots_ref[2, n]
        at = pl.ds(pl.multiple_of((slot % count) * rows, rows), rows)
        block = jnp.where(slot < count, near_ref[at, :], far_ref[at, :])
        block = jnp.where(late > 0, block[:, half:], block[:, :half]).astype(jnp.float32)
        block = (block - mean) * factor * (1.0 + mods_ref[1, place]) + mods_ref[0, place]
        out_ref[:, n * half : (n + 1) * half] = block.astype(jnp.bfloat16)


def project(modulated_ref, pieces, j):
    out, start = None, 0
    for ref in pieces:
        depth = ref.shape[1]
        term = jnp.dot(
            modulated_ref[:, start : start + depth], ref[j], preferred_element_type=jnp.float32
        )
        out = term if out is None else out + term
        start += depth
    return out


def norm_heads(out, gain_ref):
    parts = []
    for h in range(out.shape[1] // HEAD_DIM):
        part = out[:, h * HEAD_DIM : (h + 1) * HEAD_DIM]
        factor = lax.rsqrt(jnp.mean(part * part, axis=1, keepdims=True) + 1e-06)
        parts.append((part * factor * gain_ref[...]).astype(jnp.bfloat16))
    return jnp.concatenate(parts, axis=1)


def keys_kernel(modulated_ref, gain_ref, *refs):
    pieces, k_ref = refs[:-1], refs[-1]
    k_ref[...] = norm_heads(project(modulated_ref, pieces, 1), gain_ref)


def values_kernel(modulated_ref, *refs):
    pieces, v_ref = refs[:-1], refs[-1]
    v_ref[...] = project(modulated_ref, pieces, 2).astype(jnp.bfloat16)


def control_kernel(control_ref, weight_ref, bias_ref, out_ref):
    out = jnp.dot(control_ref[...], weight_ref[...], preferred_element_type=jnp.float32)
    out_ref[...] = (out + bias_ref[...]).astype(jnp.bfloat16)


def queries_kernel(modulated_ref, gain_ref, *refs):
    pieces, q_ref = refs[:-1], refs[-1]
    q_ref[...] = norm_heads(project(modulated_ref, pieces, 0), gain_ref)


def blocks_of(pieces):
    return [
        (ref, pl.ds(g * TILE, TILE)) for ref in pieces for g in range(ref.shape[0] // TILE)
    ]


def head_columns(h):
    return slice(h * HEAD_DIM, (h + 1) * HEAD_DIM)


def weigh(q_ref, allowed_ref, places_ref, first, pieces, best, total, store):
    scale = LOG2E / math.sqrt(HEAD_DIM)
    blocks = blocks_of(pieces)
    biases = [
        jnp.where(allowed_ref[places_ref[first + n]] > 0, 0.0, -1e30).astype(jnp.float32)
        for n in range(len(blocks))
    ]
    state = []
    for h in range(q_ref.shape[1] // HEAD_DIM):
        q = q_ref[:, head_columns(h)]
        scores = []
        widest = None
        for (ref, rows), bias in zip(blocks, biases, strict=True):
            part = lax.dot_general(
                q,
                ref[rows, head_columns(h)],
                (((1,), (1,)), ((), ())),
                preferred_element_type=jnp.float32,
            )
            part += bias
            scores.append(part)
            for n in range(TILE // HEAD_DIM):
                lanes = part[:, n * HEAD_DIM : (n + 1) * HEAD_DIM]
                widest = lanes if widest is None else jnp.maximum(widest, lanes)
        top = jnp.max(widest, axis=1, keepdims=True)
        if best is not None:
            top = jnp.maximum(top, best[h])
        summed = None
        for n, part in enumerate(scores):
            weights = jnp.exp2((part - top) * scale)
            for m in range(TILE // HEAD_DIM):
                lanes = weights[:, m * HEAD_DIM : (m + 1) * HEAD_DIM]
                summed = lanes if summed is None else summed + lanes
            store(h, n, weights.astype(jnp.bfloat16))
        summed = jnp.sum(summed, axis=1, keepdims=True)
        factor = None
        if best is not None:
            factor = jnp.exp2((best[h] - top) * scale)
            summed += total[h] * factor
        state.append((factor, top, summed))
    return state


def add_values(load, pieces, heads):
    sums = []
    for h in range(heads):
        out = None
        for n, (ref, rows) in enumerate(blocks_of(pieces)):
            term = jnp.dot(
                load(h, n), ref[rows, head_columns(h)], preferred_element_type=jnp.float32
            )
            out = term if out is None else out + term
        sums.append(out)
    return sums


def storing(ref):
    def store(h, n, value):
        ref[h, :, n * TILE : (n + 1) * TILE] = value

    return store


def loading(ref):
    def load(h, n):
        return ref[h, :, n * TILE : (n + 1) * TILE]

    return load


def first_kernel(count, q_ref, allowed_ref, tiles_ref, *refs):
    keys, values, (acc_ref, best_ref, total_ref) = (
        refs[:count],
        refs[count : 2 * count],
        refs[2 * count :],
    )
    kept = {}

    def store(h, n, value):
        kept[h, n] = value

    state = weigh(q_ref, allowed_ref, tiles_ref, 0, keys, None, None, store)
    for h, out in enumerate(add_values(lambda h, n: kept[h, n], values, len(state))):
        acc_ref[h] = out
        best_ref[h], total_ref[h] = state[h][1:]


def weigh_kernel(first, count, q_ref, allowed_ref, tiles_ref, *refs):
    keys = refs[:count]
    best_in, total_in, weights_ref, factor_ref, best_ref, total_ref = refs[count:]
    state = weigh(
        q_ref, allowed_ref, tiles_ref, first, keys, best_in, total_in, storing(weights_ref)
    )
    for h, new in enumerate(state):
        factor_ref[h], best_ref[h], total_ref[h] = new


def turn_kernel(first, key_count, value_count, q_ref, allowed_ref, tiles_ref, *refs):
    keys, refs = refs[:key_count], refs[key_count:]
    values, refs = refs[:value_count], refs[value_count:]
    acc_in, factor_in, weights_in, best_in, total_in, acc_ref, weights_ref, total_ref = refs
    heads = acc_in.shape[0]
    state = weigh(
        q_ref, allowed_ref, tiles_ref, first, keys, best_in, total_in, storing(weights_ref)
    )
    for h, out in enumerate(add_values(loading(weights_in), values, heads)):
        factor, _, total = state[h]
        acc_ref[h] = (acc_in[h] * factor_in[h] + out) * factor
        total_ref[h] = total


def project_out(attended, out_weight_ref, places_ref, first, ref):
    slots, _, width = ref.shape
    for k in range(slots):
        columns = pl.ds(pl.multiple_of(places_ref[first + k] * width, width), width)
        ref[k] = jnp.dot(
            attended, out_weight_ref[:, columns], preferred_element_type=jnp.float32
        ).astype(ref.dtype)


def finish_kernel(count, places_ref, out_weight_ref, acc_in, weights_in, total_in, *refs):
    values, (attended_ref, far_ref) = refs[:count], refs[count:]
    sums = add_values(loading(weights_in), values, acc_in.shape[0])
    attended = jnp.concatenate(
        [((acc_in[h] + out) / total_in[h]).astype(jnp.bfloat16) for h, out in enumerate(sums)],
        axis=1,
    )
    attended_ref[...] = attended
    project_out(attended, out_weight_ref, places_ref, far_ref.shape[0], far_ref)


def near_kernel(attended_ref, places_ref, out_weight_ref, near_ref):
    project_out(attended_ref[...], out_weight_ref, places_ref, 0, near_ref)


def cores_kernel(near_ref, far_ref, own_ref, later_ref, up_ref, down_ref):
    half = near_ref.shape[1] // 2
    first, second = slice(0, half), slice(half, 2 * half)

    def both(k, rows):
        return near_ref[k, rows, :] + far_ref[k, rows, :].astype(jnp.float32)

    for rows in (first, second):
        own_ref[rows, :] = both(0, rows)
    later_ref[first, :] = both(2, first)
    later_ref[second, :] = both(1, second)
    up_ref[first, :] = both(3, first).astype(jnp.bfloat16)
    up_ref[second, :] = both(2, second).astype(jnp.bfloat16)
    down_ref[first, :] = both(1, first).astype(jnp.bfloat16)
    down_ref[second, :] = both(3, second).astype(jnp.bfloat16)


def pick_kernel(wanted_ref, places_ref, *refs):
    half = len(refs) // 2
    rows = refs[half].shape[0]
    lane = lax.broadcasted_iota(jnp.int32, (1, rows), 1)
    for n, out_ref in enumerate(refs[half:]):
        wanted = wanted_ref[n * rows : (n + 1) * rows, :]
        total = jnp.zeros(out_ref.shape, jnp.float32)
        for k, ref in enumerate(refs[:half]):
            hit = jnp.where(wanted == lane + places_ref[k] * rows, 1.0, 0.0).astype(jnp.bfloat16)
            total += jnp.dot(hit, ref[...], preferred_element_type=jnp.float32)
        out_ref[...] = total.astype(out_ref.dtype)


def base_kernel(own_ref, gate_ref, term_ref, up_ref, down_ref, *refs):
    relayed, out_ref = refs[:-1], refs[-1]
    half = out_ref.shape[0] // 2
    wide = jnp.float32
    for rows, part_ref in ((slice(0, half), down_ref), (slice(half, 2 * half), up_ref)):
        out = own_ref[rows, :].astype(wide)
        out += gate_ref[...] * (term_ref[rows, :] + part_ref[rows, :].astype(wide))
        for ref in relayed:
            out += ref[rows, :].astype(wide)
        out_ref[rows, :] = out


def mix_kernel(base_ref, gate_ref, late_up_ref, late_down_ref, out_ref):
    half = out_ref.shape[0] // 2
    for rows, ref in ((slice(0, half), late_up_ref), (slice(half, 2 * half), late_down_ref)):
        out = base_ref[rows, :] + gate_ref[...] * ref[...].astype(jnp.float32)
        out_ref[rows, :] = out.astype(jnp.bfloat16)


def shaped(shape, dtype):
    return jax.ShapeDtypeStruct(shape, dtype)


def body(
    hidden,
    modulation,
    qkv_weight,
    q_gain,
    k_gain,
    out_weight,
    control,
    zero_weight,
    zero_bias,
    pattern,
    control_order,
):
    rows, cols = hidden.shape[1:]
    heads = cols // HEAD_DIM
    ctx_place, head_place = lax.axis_index("ctx"), lax.axis_index("head")
    x, y = ctx_place // SIDE, ctx_place % SIDE
    z, core = head_place // 2, head_place % 2
    own_rows = hidden[0]
    features = modulation.shape[2]
    mods = modulation[0].reshape(3, 2 * features // cols, 1, cols // 2)

    def ctx_of(one, two):
        return jnp.where(
            core == 0,
            ((x + one) % SIDE) * SIDE + (y + two) % SIDE,
            ((x + two) % SIDE) * SIDE + (y + one) % SIDE,
        )

    order = ctx_of(np.tile(AROUND, SIDE), np.repeat(AROUND, SIDE)).astype(jnp.int32)
    head_places = jnp.stack(
        [((z + o) % SIDE) * 2 + c for c in (core, 1 - core) for o in AROUND]
    ).astype(jnp.int32)

    place = order // 2
    away = (place // 2 - z) % SIDE
    slot = jnp.where(away == 0, 0, jnp.where(away == SIDE - 1, 1, away + 1))
    slot += jnp.where(place % 2 == core, 0, SIDE).astype(jnp.int32)
    slots = jnp.stack([slot, order % 2, order])
    listed = lax.dynamic_slice_in_dim(pattern, ctx_place, 1, 0)[0]
    allowed = jnp.any(
        listed[:, None] == jnp.arange(pattern.shape[0], dtype=jnp.int32)[None, :], axis=0
    ).astype(jnp.int32)
    wanted = jnp.concatenate(
        [
            lax.dynamic_slice_in_dim(control_order[0], ctx_of(0, o) * rows, rows, 0)
            for o in (0, 1, -1, 2)
        ]
    ).reshape(SIDE * rows, 1)
    gate = lax.dynamic_slice_in_dim(modulation[0, 2], head_place * cols, cols, 0).reshape(1, cols)

    weight = jnp.transpose(qkv_weight, (1, 0, 2))
    sides = near(z_shift, own_rows)
    ones = near(first_way, weight) + (first_way(weight, 2),)
    weights = Gather((weight,) + ones, 1)
    weights.stack, mods, slots, allowed, wanted, gate, *sides = lax.optimization_barrier(
        (weights.stack, mods, slots, allowed, wanted, gate, *sides)
    )
    weights.gather_near()
    ends = across(z_shift, *sides, 0)
    near_rows = jnp.concatenate((own_rows, *sides) + ends, axis=0)
    residual = pl.pallas_call(
        control_kernel,
        out_shape=shaped((rows, cols), jnp.bfloat16),
        in_specs=[VMEM] * 3,
        out_specs=VMEM,
        compiler_params=params(16),
        cost_estimate=cost(1),
        name="control",
    )(control[0], zero_weight, after(zero_bias, weights.stack).reshape(1, cols))
    weights.gather_across(near_rows, residual)
    far_rows = core_swap(near_rows)
    weights = weights.pieces()
    modulated = pl.pallas_call(
        modulate_kernel,
        out_shape=shaped((rows, features), jnp.bfloat16),
        in_specs=[VMEM, VMEM, VMEM, SMEM],
        out_specs=VMEM,
        compiler_params=params(20),
        cost_estimate=cost(1),
        name="modulate",
    )(near_rows, far_rows, mods, slots)

    tile = shaped((rows, cols), jnp.bfloat16)
    k = pl.pallas_call(
        keys_kernel,
        out_shape=tile,
        in_specs=[VMEM] * 7,
        out_specs=VMEM,
        compiler_params=params(20),
        cost_estimate=cost(1),
        name="keys",
    )(modulated, k_gain.reshape(1, HEAD_DIM), *weights)
    v = pl.pallas_call(
        values_kernel,
        out_shape=tile,
        in_specs=[VMEM] * 6,
        out_specs=VMEM,
        compiler_params=params(20),
        cost_estimate=cost(1),
        name="values",
    )(modulated, *weights)

    keys = Gather(first_step(k), 0)
    first_values = first_step(v)
    values = Gather(lax.optimization_barrier((*first_values, keys.stack))[:SIDE], 0)
    keys.gather_near()
    values.gather_near()
    q = pl.pallas_call(
        queries_kernel,
        out_shape=tile,
        in_specs=[VMEM] * 7,
        out_specs=VMEM,
        compiler_params=params(20),
        cost_estimate=cost(2),
        name="queries",
    )(modulated, after(q_gain, keys.stack).reshape(1, HEAD_DIM), *weights)

    sums = shaped((heads, rows, HEAD_DIM), jnp.float32)
    each = shaped((heads, rows, 1), jnp.float32)

    def weights_of(count):
        return shaped((heads, rows, count * TILE), jnp.bfloat16)

    def attention(kernel, name, time, out_shape, q, *others):
        return pl.pallas_call(
            kernel,
            out_shape=out_shape,
            in_specs=[VMEM, SMEM, SMEM] + [VMEM] * len(others),
            out_specs=[VMEM] * len(out_shape),
            compiler_params=params(16),
            cost_estimate=cost(time),
            name=name,
        )(q, allowed, order, *others)

    acc, best, total = attention(
        functools.partial(first_kernel, 1),
        "first",
        4,
        [sums, each, each],
        q,
        *keys.pieces(0, 1),
        *values.pieces(0, 1),
    )

    keys.gather_across(total)
    weights, factor, best, total = attention(
        functools.partial(weigh_kernel, 4, 2),
        "weigh",
        6,
        [weights_of(8), each, each, each],
        q,
        *keys.pieces(1, 3),
        best,
        total,
    )
    values.gather_across(total)
    residual = after(residual, total)
    residual_sides = near(first_way, residual)
    acc, weights, total = attention(
        functools.partial(turn_kernel, 12, 2, 2),
        "turn",
        6,
        [sums, weights_of(4), each],
        q,
        *keys.pieces(3, 5),
        *values.pieces(1, 3),
        acc,
        factor,
        weights,
        best,
        total,
    )
    total = after(total, *residual_sides)
    chosen = values.pieces(3, 5)
    attended, far_terms = pl.pallas_call(
        functools.partial(finish_kernel, len(chosen)),
        out_shape=[
            shaped((rows, cols), jnp.bfloat16),
            shaped((SIDE, rows, cols), jnp.bfloat16),
        ],
        in_specs=[SMEM] + [VMEM] * (4 + len(chosen)),
        out_specs=[VMEM] * 2,
        compiler_params=params(16),
        cost_estimate=cost(3),
        name="finish",
    )(head_places, out_weight, acc, weights, total, *chosen)
    near_terms = pl.pallas_call(
        near_kernel,
        out_shape=shaped((SIDE, rows, cols), jnp.float32),
        in_specs=[VMEM, SMEM, VMEM],
        out_specs=VMEM,
        compiler_params=params(16),
        cost_estimate=cost(2),
        name="near",
    )(attended, head_places, out_weight)

    own_term, later, up, down = pl.pallas_call(
        cores_kernel,
        out_shape=[shaped((rows, cols), jnp.float32)] * 2 + [shaped((rows, cols), jnp.bfloat16)] * 2,
        in_specs=[VMEM] * 2,
        out_specs=[VMEM] * 4,
        compiler_params=params(16),
        cost_estimate=cost(2),
        name="cores",
    )(near_terms, core_swap(far_terms))
    half = rows // 2
    up, down = z_shift(up, 1), z_shift(down, -1)
    wide = jnp.float32
    late_up = z_shift((later[:half] + up[:half].astype(wide)).astype(jnp.bfloat16), 1)
    late_down = z_shift((later[half:] + down[half:].astype(wide)).astype(jnp.bfloat16), -1)

    relayed = pl.pallas_call(
        pick_kernel,
        out_shape=[shaped((rows, cols), jnp.bfloat16)] * SIDE,
        in_specs=[VMEM, SMEM] + [VMEM] * SIDE,
        out_specs=[VMEM] * SIDE,
        compiler_params=params(16),
        cost_estimate=cost(5),
        name="pick",
    )(
        after(wanted, own_term),
        order,
        residual,
        *residual_sides,
        first_way(residual_sides[0], 1),
    )
    kept, *sent = relayed
    sent = second_way(sent[0], 1), second_way(sent[1], -1), second_way(sent[2], 2)

    base = pl.pallas_call(
        base_kernel,
        out_shape=shaped((rows, cols), jnp.float32),
        in_specs=[VMEM] * 9,
        out_specs=VMEM,
        compiler_params=params(16),
        cost_estimate=cost(2),
        name="base",
    )(own_rows, gate, own_term, up, down, kept, *sent)
    mixed = pl.pallas_call(
        mix_kernel,
        out_shape=shaped((rows, cols), jnp.bfloat16),
        in_specs=[VMEM] * 4,
        out_specs=VMEM,
        compiler_params=params(16),
        cost_estimate=cost(1),
        name="mix",
    )(base, gate, late_up, late_down)
    return mixed[None]


def solution(mesh):
    in_specs = (
        P("batch", "ctx", "head"),
        P("batch", None, None),
        P("ctx", None, "head"),
        P(),
        P(),
        P("head", None),
        P("batch", "ctx", None),
        P(None, "head"),
        P("head"),
        P(),
        P("batch", None),
    )
    out_specs = P("batch", "ctx", "head")
    return jax.shard_map(body, mesh=mesh, in_specs=in_specs, out_specs=out_specs, check_vma=False)
```

```python
import functools
import math

import jax
import jax.numpy as jnp
import numpy as np
from jax import lax
from jax.experimental import pallas as pl
from jax.experimental.pallas import tpu as pltpu
from jax.sharding import PartitionSpec as P

HEAD_DIM = 128
TILE = 384
SIDE = 4
AROUND = (0, -1, 1, 2)
VMEM = pl.BlockSpec(memory_space=pltpu.VMEM)
SMEM = pl.BlockSpec(memory_space=pltpu.SMEM)
HBM = pl.BlockSpec(memory_space=pl.ANY)
LOG2E = math.log2(math.e)


def cost(time):
    return pl.CostEstimate(flops=int(time * 1.15e9), bytes_accessed=0, transcendentals=0)


def params(mib):
    return pltpu.CompilerParams(vmem_limit_bytes=mib << 20)


def ctx_shift(value, axis, step):
    pairs = []
    for a in range(SIDE):
        for b in range(SIDE):
            for head in range(2 * SIDE):
                to = [a, b]
                along = (axis + head) % 2
                to[along] = (to[along] + step) % SIDE
                pairs.append(
                    ((a * SIDE + b) * 2 * SIDE + head, (to[0] * SIDE + to[1]) * 2 * SIDE + head)
                )
    return lax.ppermute(value, ("ctx", "head"), pairs)


def z_shift(value, dz):
    pairs = [(z * 2 + c, ((z + dz) % SIDE) * 2 + c) for z in range(SIDE) for c in range(2)]
    return lax.ppermute(value, "head", pairs)


def core_swap(value):
    return lax.ppermute(
        value, "head", [(z * 2 + c, z * 2 + 1 - c) for z in range(SIDE) for c in range(2)]
    )


def cut(value, axis, start, stop):
    return lax.slice_in_dim(value, start, stop, axis=axis)


def first_way(value, step):
    return ctx_shift(value, 0, step)


def second_way(value, step):
    return ctx_shift(value, 1, step)


def near(shift, value):
    return shift(value, 1), shift(value, -1)


def across(shift, back, front, axis):
    half = back.shape[axis] // 2
    return (
        shift(cut(back, axis, 0, half), 1),
        shift(cut(front, axis, half, 2 * half), -1),
    )


def after(value, *others):
    return lax.optimization_barrier((value,) + others)[0]


def first_step(value, *others):
    back, front = near(first_way, value)
    return value, back, front, first_way(after(back, *others), 1)


class Gather:
    def __init__(self, values, axis):
        self.axis = axis
        self.stack = jnp.concatenate(values, axis=axis)

    def gather_near(self, *others):
        self.back, self.front = near(second_way, after(self.stack, *others))

    def gather_across(self, *others):
        half = list(self.stack.shape)
        half[self.axis] //= 2
        out = jax.ShapeDtypeStruct(tuple(half), self.stack.dtype)
        low, high = pl.pallas_call(
            functools.partial(halves_kernel, self.axis),
            out_shape=[out, out],
            in_specs=[VMEM] * 2,
            out_specs=[VMEM] * 2,
            compiler_params=params(16),
            cost_estimate=cost(1),
            name="halves",
        )(after(self.back, *others), after(self.front, *others))
        self.first, self.second = second_way(low, 1), second_way(high, -1)

    def pieces(self, start=0, stop=5):
        return [getattr(self, name) for name in PIECES[start:stop]]


PIECES = ("stack", "back", "front", "first", "second")


def halves_kernel(axis, back_ref, front_ref, low_ref, high_ref):
    half = low_ref.shape[axis]
    low_ref[...] = back_ref[(slice(None),) * axis + (slice(0, half),)]
    high_ref[...] = front_ref[(slice(None),) * axis + (slice(half, 2 * half),)]


def modulate_kernel(near_ref, far_ref, mods_ref, slots_ref, out_ref):
    rows, width = out_ref.shape[0], near_ref.shape[1]
    count = near_ref.shape[0] // rows
    blocks = slots_ref.shape[1]
    half = out_ref.shape[1] // blocks
    total = jnp.zeros((rows, HEAD_DIM), jnp.float32)
    for ref in (near_ref, far_ref):
        for k in range(count):
            for n in range(width // HEAD_DIM):
                total += ref[
                    k * rows : (k + 1) * rows, n * HEAD_DIM : (n + 1) * HEAD_DIM
                ].astype(jnp.float32)
    mean = jnp.sum(total, axis=1, keepdims=True) / (2 * count * width)
    total = jnp.zeros((rows, HEAD_DIM), jnp.float32)
    for ref in (near_ref, far_ref):
        for k in range(count):
            for n in range(width // HEAD_DIM):
                centred = (
                    ref[k * rows : (k + 1) * rows, n * HEAD_DIM : (n + 1) * HEAD_DIM].astype(
                        jnp.float32
                    )
                    - mean
                )
                total += centred * centred
    spread = jnp.sum(total, axis=1, keepdims=True) / (2 * count * width)
    factor = lax.rsqrt(spread + 1e-06)
    for n in range(blocks):
        slot, late, place = slots_ref[0, n], slots_ref[1, n], slots_ref[2, n]
        at = pl.ds(pl.multiple_of((slot % count) * rows, rows), rows)
        block = jnp.where(slot < count, near_ref[at, :], far_ref[at, :])
        block = jnp.where(late > 0, block[:, half:], block[:, :half]).astype(jnp.float32)
        block = (block - mean) * factor * (1.0 + mods_ref[1, place]) + mods_ref[0, place]
        out_ref[:, n * half : (n + 1) * half] = block.astype(jnp.bfloat16)


def project(modulated_ref, pieces, j):
    out, start = None, 0
    for ref in pieces:
        depth = ref.shape[1]
        term = jnp.dot(
            modulated_ref[:, start : start + depth], ref[j], preferred_element_type=jnp.float32
        )
        out = term if out is None else out + term
        start += depth
    return out


def norm_heads(out, gain_ref):
    parts = []
    for h in range(out.shape[1] // HEAD_DIM):
        part = out[:, h * HEAD_DIM : (h + 1) * HEAD_DIM]
        factor = lax.rsqrt(jnp.mean(part * part, axis=1, keepdims=True) + 1e-06)
        parts.append((part * factor * gain_ref[...]).astype(jnp.bfloat16))
    return jnp.concatenate(parts, axis=1)


def keys_kernel(modulated_ref, gain_ref, *refs):
    pieces, k_ref = refs[:-1], refs[-1]
    k_ref[...] = norm_heads(project(modulated_ref, pieces, 1), gain_ref)


def values_kernel(modulated_ref, *refs):
    pieces, v_ref = refs[:-1], refs[-1]
    v_ref[...] = project(modulated_ref, pieces, 2).astype(jnp.bfloat16)


def control_kernel(control_ref, weight_ref, bias_ref, out_ref):
    out = jnp.dot(control_ref[...], weight_ref[...], preferred_element_type=jnp.float32)
    out_ref[...] = (out + bias_ref[...]).astype(jnp.bfloat16)


def queries_kernel(modulated_ref, gain_ref, *refs):
    pieces, q_ref = refs[:-1], refs[-1]
    q_ref[...] = norm_heads(project(modulated_ref, pieces, 0), gain_ref)


def blocks_of(pieces):
    return [
        (ref, pl.ds(g * TILE, TILE)) for ref in pieces for g in range(ref.shape[0] // TILE)
    ]


def head_columns(h):
    return slice(h * HEAD_DIM, (h + 1) * HEAD_DIM)


def weigh(q_ref, allowed_ref, places_ref, first, pieces, best, total, store):
    scale = LOG2E / math.sqrt(HEAD_DIM)
    blocks = blocks_of(pieces)
    biases = [
        jnp.where(allowed_ref[places_ref[first + n]] > 0, 0.0, -1e30).astype(jnp.float32)
        for n in range(len(blocks))
    ]
    state = []
    for h in range(q_ref.shape[1] // HEAD_DIM):
        q = q_ref[:, head_columns(h)]
        scores = []
        widest = None
        for (ref, rows), bias in zip(blocks, biases, strict=True):
            part = lax.dot_general(
                q,
                ref[rows, head_columns(h)],
                (((1,), (1,)), ((), ())),
                preferred_element_type=jnp.float32,
            )
            scores.append(part)
            wide = part[:, :HEAD_DIM]
            for n in range(1, TILE // HEAD_DIM):
                wide = jnp.maximum(wide, part[:, n * HEAD_DIM : (n + 1) * HEAD_DIM])
            wide += bias
            widest = wide if widest is None else jnp.maximum(widest, wide)
        top = jnp.max(widest, axis=1, keepdims=True)
        if best is not None:
            top = jnp.maximum(top, best[h])
        summed = None
        for n, part in enumerate(scores):
            weights = jnp.exp2((part - (top - biases[n])) * scale)
            for m in range(TILE // HEAD_DIM):
                lanes = weights[:, m * HEAD_DIM : (m + 1) * HEAD_DIM]
                summed = lanes if summed is None else summed + lanes
            store(h, n, weights.astype(jnp.bfloat16))
        summed = jnp.sum(summed, axis=1, keepdims=True)
        factor = None
        if best is not None:
            factor = jnp.exp2((best[h] - top) * scale)
            summed += total[h] * factor
        state.append((factor, top, summed))
    return state


def add_values(load, pieces, heads):
    sums = []
    for h in range(heads):
        out = None
        for n, (ref, rows) in enumerate(blocks_of(pieces)):
            term = jnp.dot(
                load(h, n), ref[rows, head_columns(h)], preferred_element_type=jnp.float32
            )
            out = term if out is None else out + term
        sums.append(out)
    return sums


def storing(ref):
    def store(h, n, value):
        ref[h, :, n * TILE : (n + 1) * TILE] = value

    return store


def loading(ref):
    def load(h, n):
        return ref[h, :, n * TILE : (n + 1) * TILE]

    return load


def first_kernel(count, q_ref, allowed_ref, tiles_ref, *refs):
    keys, values, (acc_ref, best_ref, total_ref) = (
        refs[:count],
        refs[count : 2 * count],
        refs[2 * count :],
    )
    kept = {}

    def store(h, n, value):
        kept[h, n] = value

    state = weigh(q_ref, allowed_ref, tiles_ref, 0, keys, None, None, store)
    for h, out in enumerate(add_values(lambda h, n: kept[h, n], values, len(state))):
        acc_ref[h] = out
        best_ref[h], total_ref[h] = state[h][1:]


def weigh_kernel(first, count, q_ref, allowed_ref, tiles_ref, *refs):
    keys = refs[:count]
    best_in, total_in, weights_ref, factor_ref, best_ref, total_ref = refs[count:]
    state = weigh(
        q_ref, allowed_ref, tiles_ref, first, keys, best_in, total_in, storing(weights_ref)
    )
    for h, new in enumerate(state):
        factor_ref[h], best_ref[h], total_ref[h] = new


def turn_kernel(first, key_count, value_count, q_ref, allowed_ref, tiles_ref, *refs):
    keys, refs = refs[:key_count], refs[key_count:]
    values, refs = refs[:value_count], refs[value_count:]
    acc_in, factor_in, weights_in, best_in, total_in, acc_ref, weights_ref, total_ref = refs
    heads = acc_in.shape[0]
    state = weigh(
        q_ref, allowed_ref, tiles_ref, first, keys, best_in, total_in, storing(weights_ref)
    )
    for h, out in enumerate(add_values(loading(weights_in), values, heads)):
        factor, _, total = state[h]
        acc_ref[h] = (acc_in[h] * factor_in[h] + out) * factor
        total_ref[h] = total


def project_out(attended, out_weight_ref, places_ref, first, ref):
    slots, _, width = ref.shape
    for k in range(slots):
        columns = pl.ds(pl.multiple_of(places_ref[first + k] * width, width), width)
        ref[k] = jnp.dot(
            attended, out_weight_ref[:, columns], preferred_element_type=jnp.float32
        ).astype(ref.dtype)


def finish_kernel(count, places_ref, out_weight_ref, acc_in, weights_in, total_in, *refs):
    values, (attended_ref, far_ref) = refs[:count], refs[count:]
    sums = add_values(loading(weights_in), values, acc_in.shape[0])
    attended = jnp.concatenate(
        [((acc_in[h] + out) / total_in[h]).astype(jnp.bfloat16) for h, out in enumerate(sums)],
        axis=1,
    )
    attended_ref[...] = attended
    project_out(attended, out_weight_ref, places_ref, far_ref.shape[0], far_ref)


def near_kernel(attended_ref, places_ref, out_weight_ref, near_ref):
    project_out(attended_ref[...], out_weight_ref, places_ref, 0, near_ref)


def cores_kernel(near_ref, far_ref, own_ref, later_ref, up_ref, down_ref):
    half = near_ref.shape[1] // 2
    first, second = slice(0, half), slice(half, 2 * half)

    def both(k, rows):
        return near_ref[k, rows, :] + far_ref[k, rows, :].astype(jnp.float32)

    for rows in (first, second):
        own_ref[rows, :] = both(0, rows)
    later_ref[first, :] = both(2, first)
    later_ref[second, :] = both(1, second)
    up_ref[first, :] = both(3, first).astype(jnp.bfloat16)
    up_ref[second, :] = both(2, second).astype(jnp.bfloat16)
    down_ref[first, :] = both(1, first).astype(jnp.bfloat16)
    down_ref[second, :] = both(3, second).astype(jnp.bfloat16)


def pick_kernel(wanted_ref, places_ref, *refs):
    half = len(refs) // 2
    rows = refs[half].shape[0]
    lane = lax.broadcasted_iota(jnp.int32, (1, rows), 1)
    for n, out_ref in enumerate(refs[half:]):
        wanted = wanted_ref[n * rows : (n + 1) * rows, :]
        total = jnp.zeros(out_ref.shape, jnp.float32)
        for k, ref in enumerate(refs[:half]):
            hit = jnp.where(wanted == lane + places_ref[k] * rows, 1.0, 0.0).astype(jnp.bfloat16)
            total += jnp.dot(hit, ref[...], preferred_element_type=jnp.float32)
        out_ref[...] = total.astype(out_ref.dtype)


def base_kernel(own_ref, gate_ref, term_ref, up_ref, down_ref, *refs):
    relayed, out_ref = refs[:-1], refs[-1]
    half = out_ref.shape[0] // 2
    wide = jnp.float32
    for rows, part_ref in ((slice(0, half), down_ref), (slice(half, 2 * half), up_ref)):
        out = own_ref[rows, :].astype(wide)
        out += gate_ref[...] * (term_ref[rows, :] + part_ref[rows, :].astype(wide))
        for ref in relayed:
            out += ref[rows, :].astype(wide)
        out_ref[rows, :] = out


def mix_kernel(base_ref, gate_ref, late_up_ref, late_down_ref, out_ref):
    half = out_ref.shape[0] // 2
    for rows, ref in ((slice(0, half), late_up_ref), (slice(half, 2 * half), late_down_ref)):
        out = base_ref[rows, :] + gate_ref[...] * ref[...].astype(jnp.float32)
        out_ref[rows, :] = out.astype(jnp.bfloat16)


def shaped(shape, dtype):
    return jax.ShapeDtypeStruct(shape, dtype)


def body(
    hidden,
    modulation,
    qkv_weight,
    q_gain,
    k_gain,
    out_weight,
    control,
    zero_weight,
    zero_bias,
    pattern,
    control_order,
):
    rows, cols = hidden.shape[1:]
    heads = cols // HEAD_DIM
    ctx_place, head_place = lax.axis_index("ctx"), lax.axis_index("head")
    x, y = ctx_place // SIDE, ctx_place % SIDE
    z, core = head_place // 2, head_place % 2
    own_rows = hidden[0]
    features = modulation.shape[2]
    mods = modulation[0].reshape(3, 2 * features // cols, 1, cols // 2)

    def ctx_of(one, two):
        return jnp.where(
            core == 0,
            ((x + one) % SIDE) * SIDE + (y + two) % SIDE,
            ((x + two) % SIDE) * SIDE + (y + one) % SIDE,
        )

    order = ctx_of(np.tile(AROUND, SIDE), np.repeat(AROUND, SIDE)).astype(jnp.int32)
    head_places = jnp.stack(
        [((z + o) % SIDE) * 2 + c for c in (core, 1 - core) for o in AROUND]
    ).astype(jnp.int32)

    place = order // 2
    away = (place // 2 - z) % SIDE
    slot = jnp.where(away == 0, 0, jnp.where(away == SIDE - 1, 1, away + 1))
    slot += jnp.where(place % 2 == core, 0, SIDE).astype(jnp.int32)
    slots = jnp.stack([slot, order % 2, order])
    listed = lax.dynamic_slice_in_dim(pattern, ctx_place, 1, 0)[0]
    allowed = jnp.any(
        listed[:, None] == jnp.arange(pattern.shape[0], dtype=jnp.int32)[None, :], axis=0
    ).astype(jnp.int32)
    wanted = jnp.concatenate(
        [
            lax.dynamic_slice_in_dim(control_order[0], ctx_of(0, o) * rows, rows, 0)
            for o in (0, 1, -1, 2)
        ]
    ).reshape(SIDE * rows, 1)
    gate = lax.dynamic_slice_in_dim(modulation[0, 2], head_place * cols, cols, 0).reshape(1, cols)

    weight = jnp.transpose(qkv_weight, (1, 0, 2))
    sides = near(z_shift, own_rows)
    ones = near(first_way, weight) + (first_way(weight, 2),)
    weights = Gather((weight,) + ones, 1)
    weights.stack, mods, slots, allowed, wanted, gate, *sides = lax.optimization_barrier(
        (weights.stack, mods, slots, allowed, wanted, gate, *sides)
    )
    weights.gather_near()
    ends = across(z_shift, *sides, 0)
    near_rows = jnp.concatenate((own_rows, *sides) + ends, axis=0)
    residual = pl.pallas_call(
        control_kernel,
        out_shape=shaped((rows, cols), jnp.bfloat16),
        in_specs=[VMEM] * 3,
        out_specs=VMEM,
        compiler_params=params(16),
        cost_estimate=cost(1),
        name="control",
    )(control[0], zero_weight, after(zero_bias, weights.stack).reshape(1, cols))
    weights.gather_across(near_rows, residual)
    far_rows = core_swap(near_rows)
    weights = weights.pieces()
    modulated = pl.pallas_call(
        modulate_kernel,
        out_shape=shaped((rows, features), jnp.bfloat16),
        in_specs=[VMEM, VMEM, VMEM, SMEM],
        out_specs=VMEM,
        compiler_params=params(20),
        cost_estimate=cost(1),
        name="modulate",
    )(near_rows, far_rows, mods, slots)

    tile = shaped((rows, cols), jnp.bfloat16)
    k = pl.pallas_call(
        keys_kernel,
        out_shape=tile,
        in_specs=[VMEM] * 7,
        out_specs=VMEM,
        compiler_params=params(20),
        cost_estimate=cost(1),
        name="keys",
    )(modulated, k_gain.reshape(1, HEAD_DIM), *weights)
    v = pl.pallas_call(
        values_kernel,
        out_shape=tile,
        in_specs=[VMEM] * 6,
        out_specs=VMEM,
        compiler_params=params(20),
        cost_estimate=cost(1),
        name="values",
    )(modulated, *weights)

    q = pl.pallas_call(
        queries_kernel,
        out_shape=tile,
        in_specs=[VMEM] * 7,
        out_specs=VMEM,
        compiler_params=params(20),
        cost_estimate=cost(2),
        name="queries",
    )(modulated, q_gain.reshape(1, HEAD_DIM), *weights)
    keys = Gather(first_step(k, q), 0)
    first_values = first_step(v)
    values = Gather(lax.optimization_barrier((*first_values, keys.stack))[:SIDE], 0)
    keys.gather_near()
    values.gather_near()

    sums = shaped((heads, rows, HEAD_DIM), jnp.float32)
    each = shaped((heads, rows, 1), jnp.float32)

    def weights_of(count):
        return shaped((heads, rows, count * TILE), jnp.bfloat16)

    def attention(kernel, name, time, out_shape, q, *others):
        return pl.pallas_call(
            kernel,
            out_shape=out_shape,
            in_specs=[VMEM, SMEM, SMEM] + [VMEM] * len(others),
            out_specs=[VMEM] * len(out_shape),
            compiler_params=params(16),
            cost_estimate=cost(time),
            name=name,
        )(q, allowed, order, *others)

    acc, best, total = attention(
        functools.partial(first_kernel, 1),
        "first",
        4,
        [sums, each, each],
        q,
        *keys.pieces(0, 1),
        *values.pieces(0, 1),
    )

    keys.gather_across(total)
    weights, factor, best, total = attention(
        functools.partial(weigh_kernel, 4, 2),
        "weigh",
        6,
        [weights_of(8), each, each, each],
        q,
        *keys.pieces(1, 3),
        best,
        total,
    )
    values.gather_across(total)
    residual = after(residual, keys.first, keys.second)
    residual_sides = near(first_way, residual)
    acc, weights, total = attention(
        functools.partial(turn_kernel, 12, 2, 2),
        "turn",
        6,
        [sums, weights_of(4), each],
        q,
        *keys.pieces(3, 5),
        *values.pieces(1, 3),
        acc,
        factor,
        weights,
        best,
        total,
    )
    total = after(total, *residual_sides)
    chosen = values.pieces(3, 5)
    attended, far_terms = pl.pallas_call(
        functools.partial(finish_kernel, len(chosen)),
        out_shape=[
            shaped((rows, cols), jnp.bfloat16),
            shaped((SIDE, rows, cols), jnp.bfloat16),
        ],
        in_specs=[SMEM] + [VMEM] * (4 + len(chosen)),
        out_specs=[VMEM] * 2,
        compiler_params=params(16),
        cost_estimate=cost(3),
        name="finish",
    )(head_places, out_weight, acc, weights, total, *chosen)
    near_terms = pl.pallas_call(
        near_kernel,
        out_shape=shaped((SIDE, rows, cols), jnp.float32),
        in_specs=[VMEM, SMEM, VMEM],
        out_specs=VMEM,
        compiler_params=params(16),
        cost_estimate=cost(2),
        name="near",
    )(attended, head_places, out_weight)

    own_term, later, up, down = pl.pallas_call(
        cores_kernel,
        out_shape=[shaped((rows, cols), jnp.float32)] * 2 + [shaped((rows, cols), jnp.bfloat16)] * 2,
        in_specs=[VMEM] * 2,
        out_specs=[VMEM] * 4,
        compiler_params=params(16),
        cost_estimate=cost(2),
        name="cores",
    )(near_terms, core_swap(far_terms))
    half = rows // 2
    up, down = z_shift(up, 1), z_shift(down, -1)
    wide = jnp.float32
    late_up = z_shift((later[:half] + up[:half].astype(wide)).astype(jnp.bfloat16), 1)
    late_down = z_shift((later[half:] + down[half:].astype(wide)).astype(jnp.bfloat16), -1)

    relayed = pl.pallas_call(
        pick_kernel,
        out_shape=[shaped((rows, cols), jnp.bfloat16)] * SIDE,
        in_specs=[VMEM, SMEM] + [VMEM] * SIDE,
        out_specs=[VMEM] * SIDE,
        compiler_params=params(16),
        cost_estimate=cost(5),
        name="pick",
    )(
        after(wanted, own_term),
        order,
        residual,
        *residual_sides,
        first_way(residual_sides[0], 1),
    )
    kept, *sent = relayed
    sent = second_way(sent[0], 1), second_way(sent[1], -1), second_way(sent[2], 2)

    base = pl.pallas_call(
        base_kernel,
        out_shape=shaped((rows, cols), jnp.float32),
        in_specs=[VMEM] * 9,
        out_specs=VMEM,
        compiler_params=params(16),
        cost_estimate=cost(2),
        name="base",
    )(own_rows, gate, own_term, up, down, kept, *sent)
    mixed = pl.pallas_call(
        mix_kernel,
        out_shape=shaped((rows, cols), jnp.bfloat16),
        in_specs=[VMEM] * 4,
        out_specs=VMEM,
        compiler_params=params(16),
        cost_estimate=cost(1),
        name="mix",
    )(base, gate, late_up, late_down)
    return mixed[None]


def solution(mesh):
    in_specs = (
        P("batch", "ctx", "head"),
        P("batch", None, None),
        P("ctx", None, "head"),
        P(),
        P(),
        P("head", None),
        P("batch", "ctx", None),
        P(None, "head"),
        P("head"),
        P(),
        P("batch", None),
    )
    out_specs = P("batch", "ctx", "head")
    return jax.shard_map(body, mesh=mesh, in_specs=in_specs, out_specs=out_specs, check_vma=False)
```

```python
import functools
import math

import jax
import jax.numpy as jnp
import numpy as np
from jax import lax
from jax.experimental import pallas as pl
from jax.experimental.pallas import tpu as pltpu
from jax.sharding import PartitionSpec as P

HEAD_DIM = 128
TILE = 384
SIDE = 4
AROUND = (0, -1, 1, 2)
VMEM = pl.BlockSpec(memory_space=pltpu.VMEM)
SMEM = pl.BlockSpec(memory_space=pltpu.SMEM)
HBM = pl.BlockSpec(memory_space=pl.ANY)
LOG2E = math.log2(math.e)


def cost(time):
    return pl.CostEstimate(flops=int(time * 1.15e9), bytes_accessed=0, transcendentals=0)


def params(mib):
    return pltpu.CompilerParams(vmem_limit_bytes=mib << 20)


def ctx_shift(value, axis, step):
    pairs = []
    for a in range(SIDE):
        for b in range(SIDE):
            for head in range(2 * SIDE):
                to = [a, b]
                along = (axis + head) % 2
                to[along] = (to[along] + step) % SIDE
                pairs.append(
                    ((a * SIDE + b) * 2 * SIDE + head, (to[0] * SIDE + to[1]) * 2 * SIDE + head)
                )
    return lax.ppermute(value, ("ctx", "head"), pairs)


def z_shift(value, dz):
    pairs = [(z * 2 + c, ((z + dz) % SIDE) * 2 + c) for z in range(SIDE) for c in range(2)]
    return lax.ppermute(value, "head", pairs)


def core_swap(value):
    return lax.ppermute(
        value, "head", [(z * 2 + c, z * 2 + 1 - c) for z in range(SIDE) for c in range(2)]
    )


def cut(value, axis, start, stop):
    return lax.slice_in_dim(value, start, stop, axis=axis)


def first_way(value, step):
    return ctx_shift(value, 0, step)


def second_way(value, step):
    return ctx_shift(value, 1, step)


def near(shift, value):
    return shift(value, 1), shift(value, -1)


def across(shift, back, front, axis):
    half = back.shape[axis] // 2
    return (
        shift(cut(back, axis, 0, half), 1),
        shift(cut(front, axis, half, 2 * half), -1),
    )


def after(value, *others):
    return lax.optimization_barrier((value,) + others)[0]


def first_step(value, *others):
    back, front = near(first_way, value)
    return value, back, front, first_way(after(back, *others), 1)


class Gather:
    def __init__(self, values, axis):
        self.axis = axis
        self.stack = jnp.concatenate(values, axis=axis)

    def gather_near(self, *others):
        self.back, self.front = near(second_way, after(self.stack, *others))

    def gather_across(self, *others):
        half = list(self.stack.shape)
        half[self.axis] //= 2
        out = jax.ShapeDtypeStruct(tuple(half), self.stack.dtype)
        low, high = pl.pallas_call(
            functools.partial(halves_kernel, self.axis),
            out_shape=[out, out],
            in_specs=[VMEM] * 2,
            out_specs=[VMEM] * 2,
            compiler_params=params(16),
            cost_estimate=cost(1),
            name="halves",
        )(after(self.back, *others), after(self.front, *others))
        self.first, self.second = second_way(low, 1), second_way(high, -1)

    def pieces(self, start=0, stop=5):
        return [getattr(self, name) for name in PIECES[start:stop]]


PIECES = ("stack", "back", "front", "first", "second")


def halves_kernel(axis, back_ref, front_ref, low_ref, high_ref):
    half = low_ref.shape[axis]
    low_ref[...] = back_ref[(slice(None),) * axis + (slice(0, half),)]
    high_ref[...] = front_ref[(slice(None),) * axis + (slice(half, 2 * half),)]


def modulate_kernel(near_ref, far_ref, mods_ref, slots_ref, out_ref):
    rows, width = out_ref.shape[0], near_ref.shape[1]
    count = near_ref.shape[0] // rows
    blocks = slots_ref.shape[1]
    half = out_ref.shape[1] // blocks
    total = jnp.zeros((rows, HEAD_DIM), jnp.float32)
    for ref in (near_ref, far_ref):
        for k in range(count):
            for n in range(width // HEAD_DIM):
                total += ref[
                    k * rows : (k + 1) * rows, n * HEAD_DIM : (n + 1) * HEAD_DIM
                ].astype(jnp.float32)
    mean = jnp.sum(total, axis=1, keepdims=True) / (2 * count * width)
    total = jnp.zeros((rows, HEAD_DIM), jnp.float32)
    for ref in (near_ref, far_ref):
        for k in range(count):
            for n in range(width // HEAD_DIM):
                centred = (
                    ref[k * rows : (k + 1) * rows, n * HEAD_DIM : (n + 1) * HEAD_DIM].astype(
                        jnp.float32
                    )
                    - mean
                )
                total += centred * centred
    spread = jnp.sum(total, axis=1, keepdims=True) / (2 * count * width)
    factor = lax.rsqrt(spread + 1e-06)
    for n in range(blocks):
        slot, late, place = slots_ref[0, n], slots_ref[1, n], slots_ref[2, n]
        at = pl.ds(pl.multiple_of((slot % count) * rows, rows), rows)
        block = jnp.where(slot < count, near_ref[at, :], far_ref[at, :])
        block = jnp.where(late > 0, block[:, half:], block[:, :half]).astype(jnp.float32)
        block = (block - mean) * factor * (1.0 + mods_ref[1, place]) + mods_ref[0, place]
        out_ref[:, n * half : (n + 1) * half] = block.astype(jnp.bfloat16)


def project(modulated_ref, pieces, j):
    out, start = None, 0
    for ref in pieces:
        depth = ref.shape[1]
        term = jnp.dot(
            modulated_ref[:, start : start + depth], ref[j], preferred_element_type=jnp.float32
        )
        out = term if out is None else out + term
        start += depth
    return out


def norm_heads(out, gain_ref):
    parts = []
    for h in range(out.shape[1] // HEAD_DIM):
        part = out[:, h * HEAD_DIM : (h + 1) * HEAD_DIM]
        factor = lax.rsqrt(jnp.mean(part * part, axis=1, keepdims=True) + 1e-06)
        parts.append((part * factor * gain_ref[...]).astype(jnp.bfloat16))
    return jnp.concatenate(parts, axis=1)


def keys_kernel(modulated_ref, gain_ref, *refs):
    pieces, k_ref = refs[:-1], refs[-1]
    k_ref[...] = norm_heads(project(modulated_ref, pieces, 1), gain_ref)


def values_kernel(modulated_ref, *refs):
    pieces, v_ref = refs[:-1], refs[-1]
    v_ref[...] = project(modulated_ref, pieces, 2).astype(jnp.bfloat16)


def control_kernel(control_ref, weight_ref, bias_ref, out_ref):
    out = jnp.dot(control_ref[...], weight_ref[...], preferred_element_type=jnp.float32)
    out_ref[...] = (out + bias_ref[...]).astype(jnp.bfloat16)


def queries_kernel(modulated_ref, gain_ref, *refs):
    pieces, q_ref = refs[:-1], refs[-1]
    q_ref[...] = norm_heads(project(modulated_ref, pieces, 0), gain_ref)


def blocks_of(pieces):
    return [
        (ref, pl.ds(g * TILE, TILE)) for ref in pieces for g in range(ref.shape[0] // TILE)
    ]


def head_columns(h):
    return slice(h * HEAD_DIM, (h + 1) * HEAD_DIM)


def weigh(q_ref, allowed_ref, places_ref, first, pieces, best, total, store):
    scale = LOG2E / math.sqrt(HEAD_DIM)
    blocks = blocks_of(pieces)
    biases = [
        jnp.where(allowed_ref[places_ref[first + n]] > 0, 0.0, -1e30).astype(jnp.float32)
        for n in range(len(blocks))
    ]
    state = []
    for h in range(q_ref.shape[1] // HEAD_DIM):
        q = q_ref[:, head_columns(h)]
        scores = []
        widest = None
        for (ref, rows), bias in zip(blocks, biases, strict=True):
            part = lax.dot_general(
                q,
                ref[rows, head_columns(h)],
                (((1,), (1,)), ((), ())),
                preferred_element_type=jnp.float32,
            )
            scores.append(part)
            wide = part[:, :HEAD_DIM]
            for n in range(1, TILE // HEAD_DIM):
                wide = jnp.maximum(wide, part[:, n * HEAD_DIM : (n + 1) * HEAD_DIM])
            wide += bias
            widest = wide if widest is None else jnp.maximum(widest, wide)
        top = jnp.max(widest, axis=1, keepdims=True)
        if best is not None:
            top = jnp.maximum(top, best[h])
        summed = None
        for n, part in enumerate(scores):
            weights = jnp.exp2((part - (top - biases[n])) * scale)
            for m in range(TILE // HEAD_DIM):
                lanes = weights[:, m * HEAD_DIM : (m + 1) * HEAD_DIM]
                summed = lanes if summed is None else summed + lanes
            store(h, n, weights.astype(jnp.bfloat16))
        summed = jnp.sum(summed, axis=1, keepdims=True)
        factor = None
        if best is not None:
            factor = jnp.exp2((best[h] - top) * scale)
            summed += total[h] * factor
        state.append((factor, top, summed))
    return state


def add_values(load, pieces, heads):
    sums = []
    for h in range(heads):
        out = None
        for n, (ref, rows) in enumerate(blocks_of(pieces)):
            term = jnp.dot(
                load(h, n), ref[rows, head_columns(h)], preferred_element_type=jnp.float32
            )
            out = term if out is None else out + term
        sums.append(out)
    return sums


def storing(ref):
    def store(h, n, value):
        ref[h, :, n * TILE : (n + 1) * TILE] = value

    return store


def loading(ref):
    def load(h, n):
        return ref[h, :, n * TILE : (n + 1) * TILE]

    return load


def first_kernel(count, q_ref, allowed_ref, tiles_ref, *refs):
    keys, values, (acc_ref, best_ref, total_ref) = (
        refs[:count],
        refs[count : 2 * count],
        refs[2 * count :],
    )
    kept = {}

    def store(h, n, value):
        kept[h, n] = value

    state = weigh(q_ref, allowed_ref, tiles_ref, 0, keys, None, None, store)
    for h, out in enumerate(add_values(lambda h, n: kept[h, n], values, len(state))):
        acc_ref[h] = out
        best_ref[h], total_ref[h] = state[h][1:]


def weigh_kernel(first, count, q_ref, allowed_ref, tiles_ref, *refs):
    keys = refs[:count]
    best_in, total_in, weights_ref, factor_ref, best_ref, total_ref = refs[count:]
    state = weigh(
        q_ref, allowed_ref, tiles_ref, first, keys, best_in, total_in, storing(weights_ref)
    )
    for h, new in enumerate(state):
        factor_ref[h], best_ref[h], total_ref[h] = new


def turn_kernel(first, key_count, value_count, q_ref, allowed_ref, tiles_ref, *refs):
    keys, refs = refs[:key_count], refs[key_count:]
    values, refs = refs[:value_count], refs[value_count:]
    acc_in, factor_in, weights_in, best_in, total_in, acc_ref, weights_ref, total_ref = refs
    heads = acc_in.shape[0]
    state = weigh(
        q_ref, allowed_ref, tiles_ref, first, keys, best_in, total_in, storing(weights_ref)
    )
    for h, out in enumerate(add_values(loading(weights_in), values, heads)):
        factor, _, total = state[h]
        acc_ref[h] = (acc_in[h] * factor_in[h] + out) * factor
        total_ref[h] = total


def project_out(attended, out_weight_ref, places_ref, first, ref):
    slots, _, width = ref.shape
    for k in range(slots):
        columns = pl.ds(pl.multiple_of(places_ref[first + k] * width, width), width)
        ref[k] = jnp.dot(
            attended, out_weight_ref[:, columns], preferred_element_type=jnp.float32
        ).astype(ref.dtype)


def finish_kernel(count, places_ref, out_weight_ref, acc_in, weights_in, total_in, *refs):
    values, (attended_ref, far_ref) = refs[:count], refs[count:]
    sums = add_values(loading(weights_in), values, acc_in.shape[0])
    attended = jnp.concatenate(
        [((acc_in[h] + out) / total_in[h]).astype(jnp.bfloat16) for h, out in enumerate(sums)],
        axis=1,
    )
    attended_ref[...] = attended
    project_out(attended, out_weight_ref, places_ref, far_ref.shape[0], far_ref)


def near_kernel(attended_ref, places_ref, out_weight_ref, near_ref):
    project_out(attended_ref[...], out_weight_ref, places_ref, 0, near_ref)


def cores_kernel(near_ref, far_ref, own_ref, later_ref, up_ref, down_ref):
    half = near_ref.shape[1] // 2
    first, second = slice(0, half), slice(half, 2 * half)

    def both(k, rows):
        return near_ref[k, rows, :] + far_ref[k, rows, :].astype(jnp.float32)

    for rows in (first, second):
        own_ref[rows, :] = both(0, rows)
    later_ref[first, :] = both(2, first)
    later_ref[second, :] = both(1, second)
    up_ref[first, :] = both(3, first).astype(jnp.bfloat16)
    up_ref[second, :] = both(2, second).astype(jnp.bfloat16)
    down_ref[first, :] = both(1, first).astype(jnp.bfloat16)
    down_ref[second, :] = both(3, second).astype(jnp.bfloat16)


def pick_kernel(wanted_ref, places_ref, *refs):
    half = len(refs) // 2
    rows = refs[half].shape[0]
    lane = lax.broadcasted_iota(jnp.int32, (1, rows), 1)
    for n, out_ref in enumerate(refs[half:]):
        wanted = wanted_ref[n * rows : (n + 1) * rows, :]
        total = jnp.zeros(out_ref.shape, jnp.float32)
        for k, ref in enumerate(refs[:half]):
            hit = jnp.where(wanted == lane + places_ref[k] * rows, 1.0, 0.0).astype(jnp.bfloat16)
            total += jnp.dot(hit, ref[...], preferred_element_type=jnp.float32)
        out_ref[...] = total.astype(out_ref.dtype)


def base_kernel(own_ref, gate_ref, term_ref, up_ref, down_ref, *refs):
    relayed, out_ref = refs[:-1], refs[-1]
    half = out_ref.shape[0] // 2
    wide = jnp.float32
    for rows, part_ref in ((slice(0, half), down_ref), (slice(half, 2 * half), up_ref)):
        out = own_ref[rows, :].astype(wide)
        out += gate_ref[...] * (term_ref[rows, :] + part_ref[rows, :].astype(wide))
        for ref in relayed:
            out += ref[rows, :].astype(wide)
        out_ref[rows, :] = out


def mix_kernel(base_ref, gate_ref, late_up_ref, late_down_ref, out_ref):
    half = out_ref.shape[0] // 2
    for rows, ref in ((slice(0, half), late_up_ref), (slice(half, 2 * half), late_down_ref)):
        out = base_ref[rows, :] + gate_ref[...] * ref[...].astype(jnp.float32)
        out_ref[rows, :] = out.astype(jnp.bfloat16)


def shaped(shape, dtype):
    return jax.ShapeDtypeStruct(shape, dtype)


def body(
    hidden,
    modulation,
    qkv_weight,
    q_gain,
    k_gain,
    out_weight,
    control,
    zero_weight,
    zero_bias,
    pattern,
    control_order,
):
    rows, cols = hidden.shape[1:]
    heads = cols // HEAD_DIM
    ctx_place, head_place = lax.axis_index("ctx"), lax.axis_index("head")
    x, y = ctx_place // SIDE, ctx_place % SIDE
    z, core = head_place // 2, head_place % 2
    own_rows = hidden[0]
    features = modulation.shape[2]
    mods = modulation[0].reshape(3, 2 * features // cols, 1, cols // 2)

    def ctx_of(one, two):
        return jnp.where(
            core == 0,
            ((x + one) % SIDE) * SIDE + (y + two) % SIDE,
            ((x + two) % SIDE) * SIDE + (y + one) % SIDE,
        )

    order = ctx_of(np.tile(AROUND, SIDE), np.repeat(AROUND, SIDE)).astype(jnp.int32)
    head_places = jnp.stack(
        [((z + o) % SIDE) * 2 + c for c in (core, 1 - core) for o in AROUND]
    ).astype(jnp.int32)

    place = order // 2
    away = (place // 2 - z) % SIDE
    slot = jnp.where(away == 0, 0, jnp.where(away == SIDE - 1, 1, away + 1))
    slot += jnp.where(place % 2 == core, 0, SIDE).astype(jnp.int32)
    slots = jnp.stack([slot, order % 2, order])
    listed = lax.dynamic_slice_in_dim(pattern, ctx_place, 1, 0)[0]
    allowed = jnp.any(
        listed[:, None] == jnp.arange(pattern.shape[0], dtype=jnp.int32)[None, :], axis=0
    ).astype(jnp.int32)
    wanted = jnp.concatenate(
        [
            lax.dynamic_slice_in_dim(control_order[0], ctx_of(0, o) * rows, rows, 0)
            for o in (0, 1, -1, 2)
        ]
    ).reshape(SIDE * rows, 1)
    gate = lax.dynamic_slice_in_dim(modulation[0, 2], head_place * cols, cols, 0).reshape(1, cols)

    weight = jnp.transpose(qkv_weight, (1, 0, 2))
    sides = near(z_shift, own_rows)
    ones = near(first_way, weight) + (first_way(weight, 2),)
    weights = Gather((weight,) + ones, 1)
    weights.stack, mods, slots, allowed, wanted, gate, *sides = lax.optimization_barrier(
        (weights.stack, mods, slots, allowed, wanted, gate, *sides)
    )
    weights.gather_near()
    ends = across(z_shift, *sides, 0)
    near_rows = jnp.concatenate((own_rows, *sides) + ends, axis=0)
    residual = pl.pallas_call(
        control_kernel,
        out_shape=shaped((rows, cols), jnp.bfloat16),
        in_specs=[VMEM] * 3,
        out_specs=VMEM,
        compiler_params=params(16),
        cost_estimate=cost(1),
        name="control",
    )(control[0], zero_weight, after(zero_bias, weights.stack).reshape(1, cols))
    weights.gather_across(near_rows, residual)
    far_rows = core_swap(near_rows)
    weights = weights.pieces()
    modulated = pl.pallas_call(
        modulate_kernel,
        out_shape=shaped((rows, features), jnp.bfloat16),
        in_specs=[VMEM, VMEM, VMEM, SMEM],
        out_specs=VMEM,
        compiler_params=params(20),
        cost_estimate=cost(1),
        name="modulate",
    )(near_rows, far_rows, mods, slots)

    tile = shaped((rows, cols), jnp.bfloat16)
    k = pl.pallas_call(
        keys_kernel,
        out_shape=tile,
        in_specs=[VMEM] * 7,
        out_specs=VMEM,
        compiler_params=params(20),
        cost_estimate=cost(1),
        name="keys",
    )(modulated, k_gain.reshape(1, HEAD_DIM), *weights)
    v = pl.pallas_call(
        values_kernel,
        out_shape=tile,
        in_specs=[VMEM] * 6,
        out_specs=VMEM,
        compiler_params=params(20),
        cost_estimate=cost(1),
        name="values",
    )(modulated, *weights)

    q = pl.pallas_call(
        queries_kernel,
        out_shape=tile,
        in_specs=[VMEM] * 7,
        out_specs=VMEM,
        compiler_params=params(20),
        cost_estimate=cost(2),
        name="queries",
    )(modulated, q_gain.reshape(1, HEAD_DIM), *weights)
    keys = Gather(first_step(k, q), 0)
    first_values = first_step(v)
    values = Gather(lax.optimization_barrier((*first_values, keys.stack))[:SIDE], 0)
    keys.gather_near()
    values.gather_near()

    sums = shaped((heads, rows, HEAD_DIM), jnp.float32)
    each = shaped((heads, rows, 1), jnp.float32)

    def weights_of(count):
        return shaped((heads, rows, count * TILE), jnp.bfloat16)

    def attention(kernel, name, time, out_shape, q, *others):
        return pl.pallas_call(
            kernel,
            out_shape=out_shape,
            in_specs=[VMEM, SMEM, SMEM] + [VMEM] * len(others),
            out_specs=[VMEM] * len(out_shape),
            compiler_params=params(16),
            cost_estimate=cost(time),
            name=name,
        )(q, allowed, order, *others)

    acc, best, total = attention(
        functools.partial(first_kernel, 1),
        "first",
        4,
        [sums, each, each],
        q,
        *keys.pieces(0, 1),
        *values.pieces(0, 1),
    )

    keys.gather_across(total)
    weights, factor, best, total = attention(
        functools.partial(weigh_kernel, 4, 2),
        "weigh",
        6,
        [weights_of(8), each, each, each],
        q,
        *keys.pieces(1, 3),
        best,
        total,
    )
    values.gather_across(total)
    residual = after(residual, keys.first, keys.second)
    residual_sides = near(first_way, residual)
    acc, weights, total = attention(
        functools.partial(turn_kernel, 12, 2, 2),
        "turn",
        6,
        [sums, weights_of(4), each],
        q,
        *keys.pieces(3, 5),
        *values.pieces(1, 3),
        acc,
        factor,
        weights,
        best,
        total,
    )
    total = after(total, residual_sides[0])
    chosen = values.pieces(3, 5)
    attended, far_terms = pl.pallas_call(
        functools.partial(finish_kernel, len(chosen)),
        out_shape=[
            shaped((rows, cols), jnp.bfloat16),
            shaped((SIDE, rows, cols), jnp.bfloat16),
        ],
        in_specs=[SMEM] + [VMEM] * (4 + len(chosen)),
        out_specs=[VMEM] * 2,
        compiler_params=params(16),
        cost_estimate=cost(3),
        name="finish",
    )(head_places, out_weight, acc, weights, total, *chosen)
    near_terms = pl.pallas_call(
        near_kernel,
        out_shape=shaped((SIDE, rows, cols), jnp.float32),
        in_specs=[VMEM, SMEM, VMEM],
        out_specs=VMEM,
        compiler_params=params(16),
        cost_estimate=cost(2),
        name="near",
    )(attended, head_places, out_weight)

    own_term, later, up, down = pl.pallas_call(
        cores_kernel,
        out_shape=[shaped((rows, cols), jnp.float32)] * 2 + [shaped((rows, cols), jnp.bfloat16)] * 2,
        in_specs=[VMEM] * 2,
        out_specs=[VMEM] * 4,
        compiler_params=params(16),
        cost_estimate=cost(2),
        name="cores",
    )(near_terms, core_swap(far_terms))
    half = rows // 2
    up, down = z_shift(up, 1), z_shift(down, -1)
    wide = jnp.float32
    late_up = z_shift((later[:half] + up[:half].astype(wide)).astype(jnp.bfloat16), 1)
    late_down = z_shift((later[half:] + down[half:].astype(wide)).astype(jnp.bfloat16), -1)

    relayed = pl.pallas_call(
        pick_kernel,
        out_shape=[shaped((rows, cols), jnp.bfloat16)] * SIDE,
        in_specs=[VMEM, SMEM] + [VMEM] * SIDE,
        out_specs=[VMEM] * SIDE,
        compiler_params=params(16),
        cost_estimate=cost(5),
        name="pick",
    )(
        after(wanted, own_term),
        order,
        residual,
        *residual_sides,
        first_way(residual_sides[0], 1),
    )
    kept, *sent = relayed
    sent = second_way(sent[0], 1), second_way(sent[1], -1), second_way(sent[2], 2)

    base = pl.pallas_call(
        base_kernel,
        out_shape=shaped((rows, cols), jnp.float32),
        in_specs=[VMEM] * 9,
        out_specs=VMEM,
        compiler_params=params(16),
        cost_estimate=cost(2),
        name="base",
    )(own_rows, gate, own_term, up, down, kept, *sent)
    mixed = pl.pallas_call(
        mix_kernel,
        out_shape=shaped((rows, cols), jnp.bfloat16),
        in_specs=[VMEM] * 4,
        out_specs=VMEM,
        compiler_params=params(16),
        cost_estimate=cost(1),
        name="mix",
    )(base, gate, late_up, late_down)
    return mixed[None]


def solution(mesh):
    in_specs = (
        P("batch", "ctx", "head"),
        P("batch", None, None),
        P("ctx", None, "head"),
        P(),
        P(),
        P("head", None),
        P("batch", "ctx", None),
        P(None, "head"),
        P("head"),
        P(),
        P("batch", None),
    )
    out_specs = P("batch", "ctx", "head")
    return jax.shard_map(body, mesh=mesh, in_specs=in_specs, out_specs=out_specs, check_vma=False)
```
